256 devices in a mesh: ps: 64 (over y, z_hi, x), patch: 4 (over z_lo, core).
Axes of the slice: x: 4, y: 4, z: 8 (z_hi: 4, z_lo: 2; z = z_hi * 2 + z_lo), core: 2. Of those that a mesh axis runs over, the one named last changes fastest.
Arguments:
- tiles: bfloat16 [64, 4, 256, 128, 128], P('ps', 'patch'), may hold values from -0.109375 to 0.109375
- tile_row: int32 [64, 4, 256], P('ps', 'patch'), may hold values from 0 to 15
- tile_col: int32 [64, 4, 256], P('ps', 'patch'), may hold values from 0 to 31
- tile_count: int32 [64, 4], P('ps', 'patch'), may hold values from 32 to 256, as said below
- slip: bfloat16 [48, 16384], P(None, 'patch'), may hold values from -6 to 6
- observations: float32 [48, 131072], P(None, 'ps'), may hold values from -6 to 6
- edge_list: int32 [2, 32768], replicated, may hold values from 0 to 16383, as said below
Outputs:
- residual: float32 [48, 131072], P(None, 'ps')
- gradient: float32 [48, 16384], P(None, ('patch', 'ps'))
The draws below stay inside these ranges and needn't reach their ends.
Inputs may be any that keep to these rules, and one draw needn't show every extreme that they name: `tile_count`: each ps index holds 256 live slots on every patch index in some draws and each draw has one such ps index; the others hold between 32 and 128. `edge_list`: edges 2 p and 2 p + 1 both have patch p as one of their ends, first or second; the other end lies 1 to 256 patches before or after p, counted cyclically over 16384; the distance 256 occurs.
All inputs are finite; a program needn't handle non-finite values.
Results may differ from the reference program's by a relative error of at most 0.0013.
Values may be sent and summed in bfloat16 or wider, within the bound.
A program may use at most 128 MiB of HBM per device.

```python
import jax
import jax.numpy as jnp
from jax import lax

BLOCK = 128
DATES = 48
KB_DEV = 32
PB_DEV = 16
REACH = 256
TCAP = 256
PATCHES = 16384
SCATTERERS = 131072
EDGES = 32768
N_PS = 64
N_PATCH = 4


def draw_tile_count(key, part):
    key = jax.random.fold_in(key, 11)
    first, second = jax.random.split(key)
    base = jax.random.randint(first, (N_PS, N_PATCH), max(TCAP // 8, 1), TCAP // 2 + 1)
    heavy = jax.random.randint(second, (), 0, N_PS)
    chosen = jnp.arange(N_PS)[:, None] == heavy
    return jnp.where(chosen, TCAP, base).astype(jnp.int32)


def draw_edge_list(key, part):
    key = jax.random.fold_in(key, 23)
    first, second, third = jax.random.split(key, 3)
    anchor = jnp.arange(EDGES) // 2
    offset = jax.random.randint(first, (EDGES,), 1, REACH + 1).at[0].set(REACH)
    sign = 2 * jax.random.randint(second, (EDGES,), 0, 2) - 1
    other = (anchor + sign * offset) % PATCHES
    order = jax.random.randint(third, (EDGES,), 0, 2)
    source = jnp.where(order == 0, anchor, other)
    target = jnp.where(order == 0, other, anchor)
    return jnp.stack([source, target]).astype(jnp.int32)


def plant(values, rng, low, high):
    shape = values.shape
    index_at = [jax.random.randint(jax.random.fold_in(rng, axis), (), 0, shape[axis]) for axis in range(len(shape))]
    values = values.at[tuple(index_at)].set(low)
    longest = shape.index(max(shape))
    index_at[longest] = (index_at[longest] + 1) % shape[longest]
    return values.at[tuple(index_at)].set(high)


def shard_levels(rng, dims, pieces, low, largest):
    level = 1.0
    for axis_at, shards_of in pieces:
        draws = jax.random.uniform(jax.random.fold_in(jax.random.fold_in(rng, 6), axis_at), (shards_of,), jnp.float32, low / len(pieces), largest / len(pieces))
        level = level * jnp.repeat(jnp.exp(draws), dims[axis_at] // shards_of).reshape((-1,) + (1,) * (len(dims) - 1 - axis_at))
    return level


def centred(own_key, extent, scale, reach, shards=(), held_as=jnp.bfloat16):
    values = jax.random.normal(own_key, extent, jnp.float32) * scale
    if len(shards) > 0:
        values = shard_levels(own_key, extent, shards, -0.22, 0.18) * values
    return jnp.clip(values, min=-reach, max=reach).astype(held_as)


def setup_inputs(seed: int = 0) -> dict:
    splits = jax.random.split(jax.random.key(seed), 8)
    return {
        "tiles": centred(splits[0], (N_PS, N_PATCH, TCAP, BLOCK, BLOCK), (BLOCK * TCAP * N_PATCH // (3 * PB_DEV)) ** -0.5, 0.109375, ((0, 64), (1, 4))),
        "tile_row": plant(jax.random.randint(splits[1], (N_PS, N_PATCH, TCAP), 0, PB_DEV), jax.random.fold_in(splits[1], 1), 0, PB_DEV - 1).astype(jnp.int32),
        "tile_col": plant(jax.random.randint(splits[2], (N_PS, N_PATCH, TCAP), 0, KB_DEV), jax.random.fold_in(splits[2], 1), 0, KB_DEV - 1).astype(jnp.int32),
        "tile_count": draw_tile_count(jax.random.fold_in(splits[7], 71), 0),
        "slip": centred(splits[4], (DATES, PATCHES), 1.0, 6.0, ((1, 4),)),
        "observations": centred(splits[5], (DATES, SCATTERERS), 1.0, 6.0, ((1, 64),), jnp.float32),
        "edge_list": draw_edge_list(jax.random.fold_in(splits[7], 71), 0),
    }


HIGH = lax.Precision.HIGHEST


def laplace(field, first, second):
    diff = field[:, first] - field[:, second]
    out = jnp.zeros_like(field)
    out = out.at[:, first].add(diff)
    return out.at[:, second].add(-diff)


def reference(tiles, tile_row, tile_col, tile_count, slip, observations, edge_list):
    rows_dev = PB_DEV * BLOCK
    slip_blocks = slip.astype(jnp.float32).reshape(DATES, N_PATCH, KB_DEV, BLOCK)
    obs_dev = observations.reshape(DATES, N_PS, rows_dev).transpose(1, 0, 2)
    patch_ids = jnp.arange(N_PATCH)[:, None]
    slot_ids = jnp.arange(TCAP)[None, :]

    def one_device(carry, inputs):
        tile_dev, row_dev, col_dev, count_dev, obs_here = inputs
        live = slot_ids < count_dev[:, None]
        tile_f = tile_dev.astype(jnp.float32)
        picked = slip_blocks[:, patch_ids, col_dev, :]
        prod = jnp.einsum('jtpk,djtk->jtdp', tile_f, picked, precision=HIGH)
        row_hot = ((row_dev[..., None] == jnp.arange(PB_DEV)) & live[..., None]).astype(jnp.float32)
        predicted = jnp.einsum('jtr,jtdp->drp', row_hot, prod, precision=HIGH).reshape(DATES, rows_dev)
        resid = predicted - obs_here
        rounded = lax.optimization_barrier(resid.astype(jnp.bfloat16)).astype(jnp.float32)
        rpick = rounded.reshape(DATES, PB_DEV, BLOCK)[:, row_dev, :]
        back = jnp.einsum('jtpk,djtp->jtdk', tile_f, rpick, precision=HIGH)
        col_hot = ((col_dev[..., None] == jnp.arange(KB_DEV)) & live[..., None]).astype(jnp.float32)
        carry = carry + jnp.einsum('jtc,jtdk->djck', col_hot, back, precision=HIGH)
        return carry, resid

    start = jnp.zeros((DATES, N_PATCH, KB_DEV, BLOCK), jnp.float32)
    data_grad, resids = lax.scan(one_device, start, (tiles, tile_row, tile_col, tile_count, obs_dev))
    residual = resids.transpose(1, 0, 2).reshape(DATES, N_PS * rows_dev)
    field = slip.astype(jnp.float32)
    smooth = laplace(field, edge_list[0], edge_list[1])
    curvature = laplace(smooth, edge_list[0], edge_list[1])
    gradient = data_grad.reshape(DATES, PATCHES) + 0.05 * curvature
    return residual, gradient
```

```python
import jax
import jax.numpy as jnp
from jax import lax
from jax.experimental import pallas as pl
from jax.experimental.pallas import tpu as pltpu
from jax.sharding import PartitionSpec as P

F32 = jnp.float32
BF16 = jnp.bfloat16
MESH = pl.DeviceIdType.MESH

BLOCK = 128
DATES = 48
SLOTS = 256
CHUNKS = 4
CH = SLOTS // CHUNKS
ROWS = 16
COLS = 32
HALF = ROWS // 2 * BLOCK
K_DEV = COLS * BLOCK
HALO = 4
WIN = 2 * HALO + 1
PATCHES = 16384
UNROLL = 8


def xor(value, m):
    if m == 0:
        return value
    if m == 1:
        return value + 1 - 2 * (value % 2)
    if m == 2:
        return (value + 2) % 4
    return 3 - value


def iota(shape, dim):
    return lax.broadcasted_iota(jnp.int32, shape, dim)


def sort_slots(row_ref, col_ref, count_ref, order, same, ends):
    shape = (SLOTS, SLOTS)
    t_lane = iota((1, SLOTS), 1)
    live = t_lane < count_ref[...]
    row = row_ref[0]
    col = col_ref[0]
    chunk_f = (t_lane // CH).astype(F32)
    t_f = t_lane.astype(F32)
    diagonal = iota(shape, 0) == iota(shape, 1)
    lane_f = iota(shape, 1).astype(F32)
    which = iota((16, SLOTS), 0)
    picker = (iota((SLOTS, 128), 0) // CH == iota((SLOTS, 128), 1)).astype(BF16)
    chunk_at = iota((COLS, 128), 1)
    for n, (mine, other, dead, limit) in enumerate(((row, col, ROWS, COLS - 1), (col, row, COLS, ROWS - 1))):
        own = jnp.where(live, mine, dead).astype(F32)
        key = (chunk_f * 64.0 + own) * SLOTS + t_f
        key_col = jnp.sum(jnp.where(diagonal, key, 0.0), axis=1, keepdims=True)
        rank = jnp.sum(jnp.where(key < key_col, 1.0, 0.0), axis=1, keepdims=True)
        one_hot = jnp.where(rank == lane_f, 1.0, 0.0).astype(BF16)
        values = jnp.where(which == 0, t_f - chunk_f * CH, jnp.where(which == 1, other.astype(F32), own))
        ordered = jnp.dot(values.astype(BF16), one_hot, preferred_element_type=F32)
        order[2 * n : 2 * n + 1, :] = jnp.clip(ordered[0:1].astype(jnp.int32), 0, CH - 1)
        order[2 * n + 1 : 2 * n + 2, :] = jnp.clip(ordered[1:2].astype(jnp.int32), 0, limit)
        key_s = ordered[2:3]
        before = pltpu.roll(jnp.broadcast_to(key_s, (8, SLOTS)), 1, 1)[0:1]
        same[n : n + 1, :] = jnp.where((key_s == before) & (t_lane % CH != 0), 1.0, 0.0)
        line = iota((COLS, SLOTS), 0).astype(F32)
        upto = jnp.dot(jnp.where(own <= line, 1.0, 0.0).astype(BF16), picker, preferred_element_type=F32)
        there = jnp.dot(jnp.where(own == line, 1.0, 0.0).astype(BF16), picker, preferred_element_type=F32)
        at = chunk_at * CH + upto.astype(jnp.int32) - 1
        ends[n * COLS : (n + 1) * COLS, :] = jnp.clip(jnp.where(there > 0.5, at, SLOTS), 0, SLOTS)


def tile_pass(n, c, tiles, left, order, same, run_ref):
    contract = (((1,), (1,)), ((), ())) if n == 0 else (((1,), (0,)), ((), ()))

    def step(g, run):
        for u in range(UNROLL):
            s = c * CH + g * UNROLL + u
            tile = tiles[order[2 * n, s]]
            lhs = left[order[2 * n + 1, s]]
            prod = lax.dot_general(lhs, tile, contract, preferred_element_type=F32)
            run = prod + run * same[n, s]
            run_ref[s] = run
        return run

    lax.fori_loop(0, CH // UNROLL, step, jnp.zeros((DATES, BLOCK), F32))


def gathered(n, line, run_ref, ends):
    total = run_ref[ends[n * COLS + line, 0]]
    for c in range(1, CHUNKS):
        total += run_ref[ends[n * COLS + line, c]]
    return total


def curvature_of(edges, window, base):
    e_at = iota((WIN, 2 * BLOCK), 1)
    block_at = (iota((WIN, 2 * BLOCK), 0) + base + 128 - HALO) % 128
    anchor = block_at * BLOCK + e_at // 2
    delta = edges[:, 0, :] + edges[:, 1, :] - 2 * anchor
    delta = (delta + 3 * PATCHES // 2 + PATCHES) % PATCHES - PATCHES // 2
    delta = jnp.concatenate([delta.astype(F32), jnp.zeros((16 - WIN, 2 * BLOCK), F32)], axis=0).astype(BF16)
    rows, cols = [], []
    for j in range(2):
        pick = (iota((2 * BLOCK, BLOCK), 0) == 2 * iota((2 * BLOCK, BLOCK), 1) + j).astype(F32).astype(BF16)
        pick_t = (iota((BLOCK, 2 * BLOCK), 1) == 2 * iota((BLOCK, 2 * BLOCK), 0) + j).astype(F32).astype(BF16)
        rows.append(jnp.dot(delta, pick, preferred_element_type=F32) + iota((16, BLOCK), 1).astype(F32))
        cols.append(
            lax.dot_general(pick_t, delta, (((1,), (1,)), ((), ())), preferred_element_type=F32)
            + iota((BLOCK, 16), 0).astype(F32)
        )
    q_at = iota((BLOCK, BLOCK), 1).astype(F32)
    p_at = iota((BLOCK, BLOCK), 0).astype(F32)
    smooth, middle, degree_mid = [], None, None
    for cq in range(HALO // 2, HALO // 2 + HALO + 1):
        blocks = []
        for cp in range(cq - 2, cq + 3):
            off = float((cq - cp) * BLOCK)
            adj = jnp.zeros((BLOCK, BLOCK), F32)
            for j in range(2):
                adj += jnp.where(cols[j][:, cp : cp + 1] == q_at + off, 1.0, 0.0)
                adj += jnp.where(rows[j][cq : cq + 1, :] == p_at - off, 1.0, 0.0)
            blocks.append(adj.astype(BF16))
        adj = jnp.concatenate(blocks, axis=0)
        around = jnp.dot(window[:, (cq - 2) * BLOCK : (cq + 3) * BLOCK], adj, preferred_element_type=F32)
        degree = around[DATES : DATES + 1]
        own = window[0:DATES, cq * BLOCK : (cq + 1) * BLOCK].astype(F32)
        smooth.append(degree * own - around[0:DATES])
        if cq == HALO:
            middle, degree_mid = adj, degree
    field = jnp.concatenate(smooth, axis=1)
    high = field.astype(BF16)
    low = (field - high.astype(F32)).astype(BF16)
    around = jnp.dot(high, middle, preferred_element_type=F32) + jnp.dot(low, middle, preferred_element_type=F32)
    return 0.05 * (degree_mid * smooth[HALO // 2] - around)


def kernel(
    tiles_h, row_h, col_h, count_h, slip_h, obs_h, edge_h, resid_h, grad_ref,
    tb0, tb1, tb2, tb3, row_v, col_v, count_v, slip_v, slip_blk, ext, obs_v, edges_v,
    order_v, same_v, ends_v, order, same, ends, run_ref,
    sib_send, sib_recv, chip_sum, zl_recv, resid_v, resid_blk, curve_v,
    rs_send, rs_recv, z_send, z_recv,
    tile_sem, in_sem, edge_sem, sm_sem, out_sem,
    sib_ss, sib_rs, halo_ss, halo_rs, zl_ss, zl_rs, res_ss, res_rs, rs_ss, rs_rs, z_ss, z_rs,
):
    ps, pt = lax.axis_index("ps"), lax.axis_index("patch")
    y, zh, x = ps // 16, ps // 4 % 4, ps % 4
    core = pt % 2
    par = x % 2
    tbs = (tb0, tb1, tb2, tb3)

    def at(yy, zz, xx):
        return (yy * 16 + zz * 4 + xx, pt)

    sibling = (ps, pt + 1 - 2 * core)
    across = (ps, (pt + 2) % 4)
    after = (ps, (pt + 1) % 4)
    before = (ps, (pt + 3) % 4)

    small = [
        pltpu.make_async_copy(row_h, row_v, in_sem.at[0]),
        pltpu.make_async_copy(col_h, col_v, in_sem.at[1]),
        pltpu.make_async_copy(count_h, count_v, in_sem.at[2]),
    ]
    slip_in = pltpu.make_async_copy(slip_h, slip_v, in_sem.at[3])
    for copy in small:
        copy.start()
    slip_in.start()
    tile_in = [
        pltpu.make_async_copy(tiles_h.at[pl.ds(c * CH, CH)], tbs[c], tile_sem.at[c]) for c in range(CHUNKS)
    ]
    for copy in tile_in:
        copy.start()
    obs_in = pltpu.make_async_copy(
        obs_h.at[:, pl.ds(pl.multiple_of(core * HALF, HALF), HALF)], obs_v, in_sem.at[4]
    )
    obs_in.start()
    base = pt * COLS + ps // 2
    edge_in = []
    for w in range(WIN):
        block = (base + 128 - HALO + w) % 128
        edge_in.append(
            pltpu.make_async_copy(
                edge_h.at[:, pl.ds(pl.multiple_of(block * 256, 256), 256)], edges_v.at[w], edge_sem.at[w]
            )
        )
    for copy in edge_in:
        copy.start()

    barrier = pltpu.get_barrier_semaphore()
    partners = [(ps, (pt + k) % 4) for k in (1, 2, 3)]
    partners += [at(xor(y, n), zh, xor(x, m)) for n in range(4) for m in range(4) if n or m]
    partners += [at(y, xor(zh, m), x) for m in (1, 2, 3)]
    for device in partners:
        pl.semaphore_signal(barrier, inc=1, device_id=device, device_id_type=MESH)

    for copy in small:
        copy.wait()
    sort_slots(row_v, col_v, count_v, order_v, same_v, ends_v)
    staged = [
        pltpu.make_async_copy(order_v, order, sm_sem.at[0]),
        pltpu.make_async_copy(same_v, same, sm_sem.at[1]),
        pltpu.make_async_copy(ends_v, ends, sm_sem.at[2]),
    ]
    for copy in staged:
        copy.start()
    slip_in.wait()
    for k in range(COLS):
        slip_blk[k] = slip_v[:, k * BLOCK : (k + 1) * BLOCK]
    ext[0:DATES, HALO * BLOCK : HALO * BLOCK + K_DEV] = slip_v[...]
    ext[DATES:, :] = jnp.ones((16, K_DEV + 2 * HALO * BLOCK), BF16)
    run_ref[SLOTS] = jnp.zeros((DATES, BLOCK), F32)
    for copy in staged:
        copy.wait()

    for c in range(CHUNKS):
        tile_in[c].wait()
        tile_pass(0, c, tbs[c], slip_blk, order, same, run_ref)

    pl.semaphore_wait(barrier, len(partners))

    def remote(src, dst, ss, rs, device):
        return pltpu.make_async_remote_copy(
            src_ref=src, dst_ref=dst, send_sem=ss, recv_sem=rs, device_id=device, device_id_type=MESH
        )

    sib = []
    for h in range(2):
        for k in range(4):
            sib_send[h, :, k * BLOCK : (k + 1) * BLOCK] = gathered(0, (1 - core) * 8 + h * 4 + k, run_ref, ends)
        sib.append(remote(sib_send.at[h], sib_recv.at[h], sib_ss.at[h], sib_rs.at[h], sibling))
        sib[h].start()
    halo = [
        remote(
            slip_v.at[:, pl.ds(K_DEV - HALO * BLOCK, HALO * BLOCK)],
            ext.at[pl.ds(0, DATES), pl.ds(0, HALO * BLOCK)],
            halo_ss.at[0], halo_rs.at[0], after,
        ),
        remote(
            slip_v.at[:, pl.ds(0, HALO * BLOCK)],
            ext.at[pl.ds(0, DATES), pl.ds(HALO * BLOCK + K_DEV, HALO * BLOCK)],
            halo_ss.at[1], halo_rs.at[1], before,
        ),
    ]
    zl = []
    for h in range(2):
        for k in range(4):
            chip_sum[h, :, k * BLOCK : (k + 1) * BLOCK] = gathered(0, core * 8 + h * 4 + k, run_ref, ends)
    for h in range(2):
        sib[h].wait_recv()
        chip_sum[h] = chip_sum[h] + sib_recv[h]
        zl.append(remote(chip_sum.at[h], zl_recv.at[h], zl_ss.at[h], zl_rs.at[h], across))
        zl[h].start()
    for copy in halo:
        copy.start()
    obs_in.wait()
    for copy in edge_in:
        copy.wait()

    res = []
    for h in range(2):
        zl[h].wait_recv()
        value = chip_sum[h] + zl_recv[h] - obs_v[:, h * 512 : (h + 1) * 512]
        at_h = core * 2 + h
        resid_v[at_h] = value
        res.append(remote(resid_v.at[at_h], resid_v.at[at_h], res_ss.at[h], res_rs.at[h], sibling))
        res[h].start()
        for k in range(4):
            resid_blk[at_h * 4 + k] = value[:, k * BLOCK : (k + 1) * BLOCK].astype(BF16)
    outs = []
    for h in range(2):
        res[h].wait_recv()
        at_h = (1 - core) * 2 + h
        value = resid_v[at_h]
        for k in range(4):
            resid_blk[at_h * 4 + k] = value[:, k * BLOCK : (k + 1) * BLOCK].astype(BF16)
    for q in range(4):
        outs.append(pltpu.make_async_copy(resid_v.at[q], resid_h.at[:, pl.ds(q * 512, 512)], out_sem.at[q]))
        outs[q].start()

    for c in range(CHUNKS):
        tile_pass(1, c, tbs[c], resid_blk, order, same, run_ref)

    low = iota((DATES, BLOCK), 1) < 64
    plane = {}
    for n in (2, 1, 3, 0):
        for mb in (2, 0):
            first = xor(y, n) * 8 + xor(x, mb) // 2
            for pair in range(2):
                b0 = gathered(1, first + 4 * pair, run_ref, ends)
                b1 = gathered(1, first + 4 * pair + 2, run_ref, ends)
                lanes = slice(pair * BLOCK, (pair + 1) * BLOCK)
                rs_send[n * 4 + mb + par, :, lanes] = jnp.where(low, b0, pltpu.roll(b1, 64, 1))
                rs_send[n * 4 + mb + 1 - par, :, lanes] = jnp.where(low, pltpu.roll(b0, 64, 1), b1)
            for m in (mb, mb + 1):
                if n or m:
                    i = n * 4 + m
                    plane[i] = remote(
                        rs_send.at[i], rs_recv.at[i], rs_ss.at[i], rs_rs.at[i], at(xor(y, n), zh, xor(x, m))
                    )
                    plane[i].start()

    for copy in halo:
        copy.wait_recv()
    window = ext[:, pl.ds(pl.multiple_of((ps // 2) * BLOCK, BLOCK), WIN * BLOCK)]
    curve_v[...] = curvature_of(edges_v, window, base)

    total = rs_send[0]
    for i in (1, 4, 3, 12, 5, 7, 13, 15, 2, 8, 6, 9, 14, 11, 10):
        plane[i].wait_recv()
        total = total + rs_recv[i]

    half = DATES // 2
    low_half = iota((half, BLOCK), 1) < 64

    def pack(block, odd):
        top, bottom = block[0:half], block[half:]
        if odd:
            return jnp.where(low_half, pltpu.roll(top, 64, 1), bottom)
        return jnp.where(low_half, top, pltpu.roll(bottom, 64, 1))

    for z in range(4):
        z_send[z] = pack(total[:, z // 2 * BLOCK : (z // 2 + 1) * BLOCK], z % 2)
    line = {}
    for m in (2, 1, 3):
        line[m] = remote(z_send.at[xor(zh, m)], z_recv.at[m], z_ss.at[m], z_rs.at[m], at(y, xor(zh, m), x))
        line[m].start()
    curve = curve_v[...]
    share = z_send[zh] + jnp.where(ps % 2 == 0, pack(curve, 0), pack(curve, 1))
    for m in (1, 3, 2):
        line[m].wait_recv()
        share = share + z_recv[m]
    grad_ref[0:half, :] = share[:, 0:64]
    grad_ref[half:, :] = pltpu.roll(share, 64, 1)[:, 0:64]

    for copy in outs:
        copy.wait()
    for copy in [*sib, *halo, *zl, *res, *plane.values(), *line.values()]:
        copy.wait_send()


def body(tiles, tile_row, tile_col, tile_count, slip, observations, edge_list):
    any_spec = pl.BlockSpec(memory_space=pltpu.HBM)
    vmem, dma = pltpu.VMEM, pltpu.SemaphoreType.DMA
    i32 = jnp.int32
    return pl.pallas_call(
        kernel,
        out_shape=(
            jax.ShapeDtypeStruct((DATES, ROWS * BLOCK), F32),
            jax.ShapeDtypeStruct((DATES, 64), F32),
        ),
        in_specs=[any_spec] * 7,
        out_specs=(any_spec, pl.BlockSpec(memory_space=vmem)),
        scratch_shapes=[
            *[vmem((CH, BLOCK, BLOCK), BF16) for _ in range(CHUNKS)],
            vmem((1, 1, SLOTS), i32),
            vmem((1, 1, SLOTS), i32),
            vmem((1, 1), i32),
            vmem((DATES, K_DEV), BF16),
            vmem((COLS, DATES, BLOCK), BF16),
            vmem((DATES + 16, K_DEV + 2 * HALO * BLOCK), BF16),
            vmem((DATES, HALF), F32),
            vmem((WIN, 2, 256), i32),
            vmem((8, SLOTS), i32),
            vmem((8, SLOTS), F32),
            vmem((2 * COLS, 128), i32),
            pltpu.SMEM((8, SLOTS), i32),
            pltpu.SMEM((8, SLOTS), F32),
            pltpu.SMEM((2 * COLS, 128), i32),
            vmem((SLOTS + 1, DATES, BLOCK), F32),
            vmem((2, DATES, 512), F32),
            vmem((2, DATES, 512), F32),
            vmem((2, DATES, 512), F32),
            vmem((2, DATES, 512), F32),
            vmem((4, DATES, 512), F32),
            vmem((ROWS, DATES, BLOCK), BF16),
            vmem((DATES, BLOCK), F32),
            vmem((16, DATES, 256), F32),
            vmem((16, DATES, 256), F32),
            vmem((4, DATES // 2, BLOCK), F32),
            vmem((4, DATES // 2, BLOCK), F32),
            dma((CHUNKS,)), dma((5,)), dma((WIN,)), dma((3,)), dma((4,)),
            dma((2,)), dma((2,)), dma((2,)), dma((2,)), dma((2,)), dma((2,)), dma((2,)), dma((2,)),
            dma((16,)), dma((16,)), dma((4,)), dma((4,)),
        ],
        compiler_params=pltpu.CompilerParams(
            collective_id=0, has_side_effects=True, vmem_limit_bytes=48 * 2**20
        ),
        cost_estimate=pl.CostEstimate(flops=2 * 10**9, bytes_accessed=10 * 2**20, transcendentals=0),
    )(tiles[0, 0], tile_row, tile_col, tile_count, slip, observations, edge_list)


def solution(mesh):
    in_specs = (
        P("ps", "patch", None, None, None),
        P("ps", "patch", None),
        P("ps", "patch", None),
        P("ps", "patch"),
        P(None, "patch"),
        P(None, "ps"),
        P(),
    )
    out_specs = (P(None, "ps"), P(None, ("patch", "ps")))
    return jax.shard_map(body, mesh=mesh, in_specs=in_specs, out_specs=out_specs, check_vma=False)
```

```python
import functools

import jax
import jax.numpy as jnp
from jax import lax
from jax.experimental import pallas as pl
from jax.experimental.pallas import tpu as pltpu
from jax.sharding import PartitionSpec as P

F32 = jnp.float32
BF16 = jnp.bfloat16
MESH = pl.DeviceIdType.MESH

BLOCK = 128
DATES = 48
SLOTS = 256
CHUNKS = 2
CH = SLOTS // CHUNKS
ROWS = 16
COLS = 32
HALF = ROWS // 2 * BLOCK
K_DEV = COLS * BLOCK
HALO = 4
WIN = 2 * HALO + 1
PATCHES = 16384
UNROLL = 64


def xor(value, m):
    if m == 0:
        return value
    if m == 1:
        return value + 1 - 2 * (value % 2)
    if m == 2:
        return (value + 2) % 4
    return 3 - value


def iota(shape, dim):
    return lax.broadcasted_iota(jnp.int32, shape, dim)


def sort_slots(row_ref, col_ref, count_ref, order, same, ends):
    shape = (SLOTS, SLOTS)
    t_lane = iota((1, SLOTS), 1)
    live = t_lane < count_ref[...]
    row = row_ref[0]
    col = col_ref[0]
    chunk_f = (t_lane // CH).astype(F32)
    t_f = t_lane.astype(F32)
    diagonal = iota(shape, 0) == iota(shape, 1)
    lane_f = iota(shape, 1).astype(F32)
    which = iota((16, SLOTS), 0)
    picker = (iota((SLOTS, 128), 0) // CH == iota((SLOTS, 128), 1)).astype(BF16)
    chunk_at = iota((COLS, 128), 1)
    for n, (mine, other, dead, limit) in enumerate(((row, col, ROWS, COLS - 1), (col, row, COLS, ROWS - 1))):
        own = jnp.where(live, mine, dead).astype(F32)
        key = (chunk_f * 64.0 + own) * SLOTS + t_f
        key_col = jnp.sum(jnp.where(diagonal, key, 0.0), axis=1, keepdims=True)
        rank = jnp.sum(jnp.where(key < key_col, 1.0, 0.0), axis=1, keepdims=True)
        one_hot = jnp.where(rank == lane_f, 1.0, 0.0).astype(BF16)
        values = jnp.where(which == 0, t_f - chunk_f * CH, jnp.where(which == 1, other.astype(F32), own))
        ordered = jnp.dot(values.astype(BF16), one_hot, preferred_element_type=F32)
        order[2 * n : 2 * n + 1, :] = jnp.clip(ordered[0:1].astype(jnp.int32), 0, CH - 1)
        order[2 * n + 1 : 2 * n + 2, :] = jnp.clip(ordered[1:2].astype(jnp.int32), 0, limit)
        key_s = ordered[2:3]
        before = pltpu.roll(jnp.broadcast_to(key_s, (8, SLOTS)), 1, 1)[0:1]
        same[n : n + 1, :] = jnp.where((key_s == before) & (t_lane % CH != 0), 1.0, 0.0)
        line = iota((COLS, SLOTS), 0).astype(F32)
        upto = jnp.dot(jnp.where(own <= line, 1.0, 0.0).astype(BF16), picker, preferred_element_type=F32)
        there = jnp.dot(jnp.where(own == line, 1.0, 0.0).astype(BF16), picker, preferred_element_type=F32)
        at = chunk_at * CH + upto.astype(jnp.int32) - 1
        ends[n * COLS : (n + 1) * COLS, :] = jnp.clip(jnp.where(there > 0.5, at, SLOTS), 0, SLOTS)


def tile_pass(n, c, tiles, left, order, same, run_ref):
    zeros = jnp.zeros((DATES, BLOCK), BF16)
    contract = (((1,), (1,)), ((), ())) if n == 0 else (((1,), (0,)), ((), ()))

    def step(g, run):
        for u in range(0, UNROLL, 2):
            s = c * CH + g * UNROLL + u
            pair = jnp.concatenate([tiles[order[2 * n, s]], tiles[order[2 * n, s + 1]]], axis=1 - n)
            lhs = jnp.concatenate(
                [
                    jnp.concatenate([left[order[2 * n + 1, s]], zeros], axis=1),
                    jnp.concatenate([zeros, left[order[2 * n + 1, s + 1]]], axis=1),
                ],
                axis=0,
            )
            prod = lax.dot_general(lhs, pair, contract, preferred_element_type=F32)
            run = prod[0:DATES] + run * same[n, s]
            run_ref[s] = run
            run = prod[DATES:] + run * same[n, s + 1]
            run_ref[s + 1] = run
        return run

    lax.fori_loop(0, CH // UNROLL, step, jnp.zeros((DATES, BLOCK), F32))


def gathered(n, line, run_ref, ends):
    total = run_ref[ends[n * COLS + line, 0]]
    for c in range(1, CHUNKS):
        total += run_ref[ends[n * COLS + line, c]]
    return total


def curvature_of(edges, window, base):
    e_at = iota((WIN, 2 * BLOCK), 1)
    block_at = (iota((WIN, 2 * BLOCK), 0) + base + 128 - HALO) % 128
    anchor = block_at * BLOCK + e_at // 2
    delta = edges[:, 0, :] + edges[:, 1, :] - 2 * anchor
    delta = (delta + 3 * PATCHES // 2 + PATCHES) % PATCHES - PATCHES // 2
    delta = jnp.concatenate([delta.astype(F32), jnp.zeros((16 - WIN, 2 * BLOCK), F32)], axis=0).astype(BF16)
    rows, cols = [], []
    for j in range(2):
        pick = (iota((2 * BLOCK, BLOCK), 0) == 2 * iota((2 * BLOCK, BLOCK), 1) + j).astype(F32).astype(BF16)
        pick_t = (iota((BLOCK, 2 * BLOCK), 1) == 2 * iota((BLOCK, 2 * BLOCK), 0) + j).astype(F32).astype(BF16)
        rows.append(jnp.dot(delta, pick, preferred_element_type=F32) + iota((16, BLOCK), 1).astype(F32))
        cols.append(
            lax.dot_general(pick_t, delta, (((1,), (1,)), ((), ())), preferred_element_type=F32)
            + iota((BLOCK, 16), 0).astype(F32)
        )
    q_at = iota((BLOCK, BLOCK), 1).astype(F32)
    p_at = iota((BLOCK, BLOCK), 0).astype(F32)
    smooth, middle, degree_mid = [], None, None
    for cq in range(HALO // 2, HALO // 2 + HALO + 1):
        blocks = []
        for cp in range(cq - 2, cq + 3):
            off = float((cq - cp) * BLOCK)
            adj = jnp.zeros((BLOCK, BLOCK), F32)
            for j in range(2):
                adj += jnp.where(cols[j][:, cp : cp + 1] == q_at + off, 1.0, 0.0)
                adj += jnp.where(rows[j][cq : cq + 1, :] == p_at - off, 1.0, 0.0)
            blocks.append(adj.astype(BF16))
        adj = jnp.concatenate(blocks, axis=0)
        around = jnp.dot(window[:, (cq - 2) * BLOCK : (cq + 3) * BLOCK], adj, preferred_element_type=F32)
        degree = around[DATES : DATES + 1]
        own = window[0:DATES, cq * BLOCK : (cq + 1) * BLOCK].astype(F32)
        smooth.append(degree * own - around[0:DATES])
        if cq == HALO:
            middle, degree_mid = adj, degree
    field = jnp.concatenate(smooth, axis=1)
    high = field.astype(BF16)
    low = (field - high.astype(F32)).astype(BF16)
    around = jnp.dot(high, middle, preferred_element_type=F32) + jnp.dot(low, middle, preferred_element_type=F32)
    return 0.05 * (degree_mid * smooth[HALO // 2] - around)


def kernel(
    tiles_h, row_h, col_h, count_h, slip_h, obs_h, edge_h, resid_h, grad_ref,
    tb0, tb1, row_v, col_v, count_v, slip_v, slip_blk, ext, obs_v, edges_v,
    order_v, same_v, ends_v, order, same, ends, run_ref,
    sib_send, sib_recv, chip_sum, zl_recv, resid_v, resid_blk, curve_v,
    rs_send, rs_recv, z_send, z_recv,
    tile_sem, in_sem, edge_sem, sm_sem, out_sem,
    sib_ss, sib_rs, halo_ss, halo_rs, zl_ss, zl_rs, res_ss, res_rs, rs_ss, rs_rs, z_ss, z_rs,
):
    ps, pt = lax.axis_index("ps"), lax.axis_index("patch")
    y, zh, x = ps // 16, ps // 4 % 4, ps % 4
    core = pt % 2
    par = x % 2
    tbs = (tb0, tb1)

    def at(yy, zz, xx):
        return (yy * 16 + zz * 4 + xx, pt)

    sibling = (ps, pt + 1 - 2 * core)
    across = (ps, (pt + 2) % 4)
    after = (ps, (pt + 1) % 4)
    before = (ps, (pt + 3) % 4)

    small = [
        pltpu.make_async_copy(row_h, row_v, in_sem.at[0]),
        pltpu.make_async_copy(col_h, col_v, in_sem.at[1]),
        pltpu.make_async_copy(count_h, count_v, in_sem.at[2]),
    ]
    slip_in = pltpu.make_async_copy(slip_h, slip_v, in_sem.at[3])
    for copy in small:
        copy.start()
    slip_in.start()
    tile_in = [
        pltpu.make_async_copy(tiles_h.at[pl.ds(c * CH, CH)], tbs[c], tile_sem.at[c]) for c in range(CHUNKS)
    ]
    for copy in tile_in:
        copy.start()
    obs_in = pltpu.make_async_copy(
        obs_h.at[:, pl.ds(pl.multiple_of(core * HALF, HALF), HALF)], obs_v, in_sem.at[4]
    )
    obs_in.start()
    base = pt * COLS + ps // 2
    edge_in = []
    for w in range(WIN):
        block = (base + 128 - HALO + w) % 128
        edge_in.append(
            pltpu.make_async_copy(
                edge_h.at[:, pl.ds(pl.multiple_of(block * 256, 256), 256)], edges_v.at[w], edge_sem.at[w]
            )
        )
    for copy in edge_in:
        copy.start()

    barrier = pltpu.get_barrier_semaphore()
    partners = [(ps, (pt + k) % 4) for k in (1, 2, 3)]
    partners += [at(xor(y, n), zh, xor(x, m)) for n in range(4) for m in range(4) if n or m]
    partners += [at(y, xor(zh, m), x) for m in (1, 2, 3)]
    for device in partners:
        pl.semaphore_signal(barrier, inc=1, device_id=device, device_id_type=MESH)

    for copy in small:
        copy.wait()
    sort_slots(row_v, col_v, count_v, order_v, same_v, ends_v)
    staged = [
        pltpu.make_async_copy(order_v, order, sm_sem.at[0]),
        pltpu.make_async_copy(same_v, same, sm_sem.at[1]),
        pltpu.make_async_copy(ends_v, ends, sm_sem.at[2]),
    ]
    for copy in staged:
        copy.start()
    slip_in.wait()
    for k in range(COLS):
        slip_blk[k] = slip_v[:, k * BLOCK : (k + 1) * BLOCK]
    ext[0:DATES, HALO * BLOCK : HALO * BLOCK + K_DEV] = slip_v[...]
    ext[DATES:, :] = jnp.ones((16, K_DEV + 2 * HALO * BLOCK), BF16)
    run_ref[SLOTS] = jnp.zeros((DATES, BLOCK), F32)
    for copy in staged:
        copy.wait()

    for c in range(CHUNKS):
        tile_in[c].wait()
        tile_pass(0, c, tbs[c], slip_blk, order, same, run_ref)

    pl.semaphore_wait(barrier, len(partners))

    def remote(src, dst, ss, rs, device):
        return pltpu.make_async_remote_copy(
            src_ref=src, dst_ref=dst, send_sem=ss, recv_sem=rs, device_id=device, device_id_type=MESH
        )

    sib = []
    for h in range(2):
        for k in range(4):
            sib_send[h, :, k * BLOCK : (k + 1) * BLOCK] = gathered(0, (1 - core) * 8 + h * 4 + k, run_ref, ends)
        sib.append(remote(sib_send.at[h], sib_recv.at[h], sib_ss.at[h], sib_rs.at[h], sibling))
        sib[h].start()
    halo = [
        remote(
            slip_v.at[:, pl.ds(K_DEV - HALO * BLOCK, HALO * BLOCK)],
            ext.at[pl.ds(0, DATES), pl.ds(0, HALO * BLOCK)],
            halo_ss.at[0], halo_rs.at[0], after,
        ),
        remote(
            slip_v.at[:, pl.ds(0, HALO * BLOCK)],
            ext.at[pl.ds(0, DATES), pl.ds(HALO * BLOCK + K_DEV, HALO * BLOCK)],
            halo_ss.at[1], halo_rs.at[1], before,
        ),
    ]
    zl = []
    for h in range(2):
        for k in range(4):
            chip_sum[h, :, k * BLOCK : (k + 1) * BLOCK] = gathered(0, core * 8 + h * 4 + k, run_ref, ends)
    for h in range(2):
        sib[h].wait_recv()
        chip_sum[h] = chip_sum[h] + sib_recv[h]
        zl.append(remote(chip_sum.at[h], zl_recv.at[h], zl_ss.at[h], zl_rs.at[h], across))
        zl[h].start()
    for copy in halo:
        copy.start()
    obs_in.wait()
    for copy in edge_in:
        copy.wait()

    res = []
    for h in range(2):
        zl[h].wait_recv()
        value = chip_sum[h] + zl_recv[h] - obs_v[:, h * 512 : (h + 1) * 512]
        at_h = core * 2 + h
        resid_v[at_h] = value
        res.append(remote(resid_v.at[at_h], resid_v.at[at_h], res_ss.at[h], res_rs.at[h], sibling))
        res[h].start()
        for k in range(4):
            resid_blk[at_h * 4 + k] = value[:, k * BLOCK : (k + 1) * BLOCK].astype(BF16)
    outs = []
    for h in range(2):
        res[h].wait_recv()
        at_h = (1 - core) * 2 + h
        value = resid_v[at_h]
        for k in range(4):
            resid_blk[at_h * 4 + k] = value[:, k * BLOCK : (k + 1) * BLOCK].astype(BF16)
    for q in range(4):
        outs.append(pltpu.make_async_copy(resid_v.at[q], resid_h.at[:, pl.ds(q * 512, 512)], out_sem.at[q]))
        outs[q].start()

    for c in range(CHUNKS):
        tile_pass(1, c, tbs[c], resid_blk, order, same, run_ref)

    low = iota((DATES, BLOCK), 1) < 64
    plane = {}
    for n in (2, 1, 3, 0):
        for mb in (2, 0):
            first = xor(y, n) * 8 + xor(x, mb) // 2
            for pair in range(2):
                b0 = gathered(1, first + 4 * pair, run_ref, ends)
                b1 = gathered(1, first + 4 * pair + 2, run_ref, ends)
                lanes = slice(pair * BLOCK, (pair + 1) * BLOCK)
                rs_send[n * 4 + mb + par, :, lanes] = jnp.where(low, b0, pltpu.roll(b1, 64, 1))
                rs_send[n * 4 + mb + 1 - par, :, lanes] = jnp.where(low, pltpu.roll(b0, 64, 1), b1)
            for m in (mb, mb + 1):
                if n or m:
                    i = n * 4 + m
                    plane[i] = remote(
                        rs_send.at[i], rs_recv.at[i], rs_ss.at[i], rs_rs.at[i], at(xor(y, n), zh, xor(x, m))
                    )
                    plane[i].start()

    for copy in halo:
        copy.wait_recv()
    window = ext[:, pl.ds(pl.multiple_of((ps // 2) * BLOCK, BLOCK), WIN * BLOCK)]
    curve_v[...] = curvature_of(edges_v, window, base)

    total = rs_send[0]
    for i in (1, 4, 3, 12, 5, 7, 13, 15, 2, 8, 6, 9, 14, 11, 10):
        plane[i].wait_recv()
        total = total + rs_recv[i]

    half = DATES // 2
    low_half = iota((half, BLOCK), 1) < 64

    def pack(block, odd):
        top, bottom = block[0:half], block[half:]
        if odd:
            return jnp.where(low_half, pltpu.roll(top, 64, 1), bottom)
        return jnp.where(low_half, top, pltpu.roll(bottom, 64, 1))

    for z in range(4):
        z_send[z] = pack(total[:, z // 2 * BLOCK : (z // 2 + 1) * BLOCK], z % 2)
    line = {}
    for m in (2, 1, 3):
        line[m] = remote(z_send.at[xor(zh, m)], z_recv.at[m], z_ss.at[m], z_rs.at[m], at(y, xor(zh, m), x))
        line[m].start()
    curve = curve_v[...]
    share = z_send[zh] + jnp.where(ps % 2 == 0, pack(curve, 0), pack(curve, 1))
    for m in (1, 3, 2):
        line[m].wait_recv()
        share = share + z_recv[m]
    grad_ref[0:half, :] = share[:, 0:64]
    grad_ref[half:, :] = pltpu.roll(share, 64, 1)[:, 0:64]

    for copy in outs:
        copy.wait()
    for copy in [*sib, *halo, *zl, *res, *plane.values(), *line.values()]:
        copy.wait_send()


def body(tiles, tile_row, tile_col, tile_count, slip, observations, edge_list):
    any_spec = pl.BlockSpec(memory_space=pltpu.HBM)
    vmem, dma = pltpu.VMEM, pltpu.SemaphoreType.DMA
    i32 = jnp.int32
    near = functools.partial(pltpu.with_memory_space_constraint, memory_space=pltpu.HBM)
    return pl.pallas_call(
        kernel,
        out_shape=(
            jax.ShapeDtypeStruct((DATES, ROWS * BLOCK), F32),
            jax.ShapeDtypeStruct((DATES, 64), F32),
        ),
        in_specs=[any_spec] * 7,
        out_specs=(any_spec, pl.BlockSpec(memory_space=vmem)),
        scratch_shapes=[
            *[vmem((CH, BLOCK, BLOCK), BF16) for _ in range(CHUNKS)],
            vmem((1, 1, SLOTS), i32),
            vmem((1, 1, SLOTS), i32),
            vmem((1, 1), i32),
            vmem((DATES, K_DEV), BF16),
            vmem((COLS, DATES, BLOCK), BF16),
            vmem((DATES + 16, K_DEV + 2 * HALO * BLOCK), BF16),
            vmem((DATES, HALF), F32),
            vmem((WIN, 2, 256), i32),
            vmem((8, SLOTS), i32),
            vmem((8, SLOTS), F32),
            vmem((2 * COLS, 128), i32),
            pltpu.SMEM((8, SLOTS), i32),
            pltpu.SMEM((8, SLOTS), F32),
            pltpu.SMEM((2 * COLS, 128), i32),
            vmem((SLOTS + 1, DATES, BLOCK), F32),
            vmem((2, DATES, 512), F32),
            vmem((2, DATES, 512), F32),
            vmem((2, DATES, 512), F32),
            vmem((2, DATES, 512), F32),
            vmem((4, DATES, 512), F32),
            vmem((ROWS, DATES, BLOCK), BF16),
            vmem((DATES, BLOCK), F32),
            vmem((16, DATES, 256), F32),
            vmem((16, DATES, 256), F32),
            vmem((4, DATES // 2, BLOCK), F32),
            vmem((4, DATES // 2, BLOCK), F32),
            dma((CHUNKS,)), dma((5,)), dma((WIN,)), dma((3,)), dma((4,)),
            dma((2,)), dma((2,)), dma((2,)), dma((2,)), dma((2,)), dma((2,)), dma((2,)), dma((2,)),
            dma((16,)), dma((16,)), dma((4,)), dma((4,)),
        ],
        compiler_params=pltpu.CompilerParams(
            collective_id=0, has_side_effects=True, vmem_limit_bytes=48 * 2**20
        ),
        cost_estimate=pl.CostEstimate(flops=2 * 10**9, bytes_accessed=10 * 2**20, transcendentals=0),
    )(
        *(near(a) for a in (tiles[0, 0], tile_row, tile_col)),
        tile_count,
        *(near(a) for a in (slip, observations, edge_list)),
    )


def solution(mesh):
    in_specs = (
        P("ps", "patch", None, None, None),
        P("ps", "patch", None),
        P("ps", "patch", None),
        P("ps", "patch"),
        P(None, "patch"),
        P(None, "ps"),
        P(),
    )
    out_specs = (P(None, "ps"), P(None, ("patch", "ps")))
    return jax.shard_map(body, mesh=mesh, in_specs=in_specs, out_specs=out_specs, check_vma=False)
```

```python
import functools

import jax
import jax.numpy as jnp
from jax import lax
from jax.experimental import pallas as pl
from jax.experimental.pallas import tpu as pltpu
from jax.sharding import PartitionSpec as P

F32 = jnp.float32
BF16 = jnp.bfloat16
MESH = pl.DeviceIdType.MESH

BLOCK = 128
DATES = 48
SLOTS = 256
CHUNKS = 2
CH = SLOTS // CHUNKS
ROWS = 16
COLS = 32
HALF = ROWS // 2 * BLOCK
K_DEV = COLS * BLOCK
HALO = 4
WIN = 2 * HALO + 1
PATCHES = 16384
UNROLL = 64
GROUPS = ((0, 16), (16, 32))


def xor(value, m):
    if m == 0:
        return value
    if m == 1:
        return value + 1 - 2 * (value % 2)
    if m == 2:
        return (value + 2) % 4
    return 3 - value


def iota(shape, dim):
    return lax.broadcasted_iota(jnp.int32, shape, dim)


def sort_slots(row_ref, col_ref, count_ref, order, same, ends):
    shape = (SLOTS, SLOTS)
    t_lane = iota((1, SLOTS), 1)
    live = t_lane < count_ref[...]
    row = row_ref[0]
    col = col_ref[0]
    chunk_f = (t_lane // CH).astype(F32)
    t_f = t_lane.astype(F32)
    diagonal = iota(shape, 0) == iota(shape, 1)
    lane_f = iota(shape, 1).astype(F32)
    which = iota((16, SLOTS), 0)
    picker = (iota((SLOTS, 128), 0) // CH == iota((SLOTS, 128), 1)).astype(BF16)
    chunk_at = iota((COLS, 128), 1)
    for n, (mine, other, dead, limit) in enumerate(((row, col, ROWS, COLS - 1), (col, row, COLS, ROWS - 1))):
        own = jnp.where(live, mine, dead).astype(F32)
        key = (chunk_f * 64.0 + own) * SLOTS + t_f
        key_col = jnp.sum(jnp.where(diagonal, key, 0.0), axis=1, keepdims=True)
        rank = jnp.sum(jnp.where(key < key_col, 1.0, 0.0), axis=1, keepdims=True)
        one_hot = jnp.where(rank == lane_f, 1.0, 0.0).astype(BF16)
        values = jnp.where(which == 0, t_f - chunk_f * CH, jnp.where(which == 1, other.astype(F32), own))
        ordered = jnp.dot(values.astype(BF16), one_hot, preferred_element_type=F32)
        order[2 * n : 2 * n + 1, :] = jnp.clip(ordered[0:1].astype(jnp.int32), 0, CH - 1)
        order[2 * n + 1 : 2 * n + 2, :] = jnp.clip(ordered[1:2].astype(jnp.int32), 0, limit)
        key_s = ordered[2:3]
        before = pltpu.roll(jnp.broadcast_to(key_s, (8, SLOTS)), 1, 1)[0:1]
        same[n : n + 1, :] = jnp.where((key_s == before) & (t_lane % CH != 0), 1.0, 0.0)
        line = iota((COLS, SLOTS), 0).astype(F32)
        upto = jnp.dot(jnp.where(own <= line, 1.0, 0.0).astype(BF16), picker, preferred_element_type=F32)
        there = jnp.dot(jnp.where(own == line, 1.0, 0.0).astype(BF16), picker, preferred_element_type=F32)
        at = chunk_at * CH + upto.astype(jnp.int32) - 1
        ends[n * COLS : (n + 1) * COLS, :] = jnp.clip(jnp.where(there > 0.5, at, SLOTS), 0, SLOTS)


def tile_pass(n, c, tiles, left, order, same, run_ref, first=0, dates=DATES):
    zeros = jnp.zeros((dates, BLOCK), BF16)
    lines = slice(first, first + dates)
    contract = (((1,), (1,)), ((), ())) if n == 0 else (((1,), (0,)), ((), ()))

    def step(g, run):
        for u in range(0, UNROLL, 2):
            s = c * CH + g * UNROLL + u
            pair = jnp.concatenate([tiles[order[2 * n, s]], tiles[order[2 * n, s + 1]]], axis=1 - n)
            lhs = jnp.concatenate(
                [
                    jnp.concatenate([left[order[2 * n + 1, s]], zeros], axis=1),
                    jnp.concatenate([zeros, left[order[2 * n + 1, s + 1]]], axis=1),
                ],
                axis=0,
            )
            prod = lax.dot_general(lhs, pair, contract, preferred_element_type=F32)
            run = prod[0:dates] + run * same[n, s]
            run_ref[s, lines] = run
            run = prod[dates:] + run * same[n, s + 1]
            run_ref[s + 1, lines] = run
        return run

    lax.fori_loop(0, CH // UNROLL, step, jnp.zeros((dates, BLOCK), F32))


def gathered(n, line, run_ref, ends, first, dates):
    lines = slice(first, first + dates)
    total = run_ref[ends[n * COLS + line, 0], lines]
    for c in range(1, CHUNKS):
        total += run_ref[ends[n * COLS + line, c], lines]
    return total


def curvature_of(edges, window, base):
    e_at = iota((WIN, 2 * BLOCK), 1)
    block_at = (iota((WIN, 2 * BLOCK), 0) + base + 128 - HALO) % 128
    anchor = block_at * BLOCK + e_at // 2
    delta = edges[:, 0, :] + edges[:, 1, :] - 2 * anchor
    delta = (delta + 3 * PATCHES // 2 + PATCHES) % PATCHES - PATCHES // 2
    delta = jnp.concatenate([delta.astype(F32), jnp.zeros((16 - WIN, 2 * BLOCK), F32)], axis=0).astype(BF16)
    rows, cols = [], []
    for j in range(2):
        pick = (iota((2 * BLOCK, BLOCK), 0) == 2 * iota((2 * BLOCK, BLOCK), 1) + j).astype(F32).astype(BF16)
        pick_t = (iota((BLOCK, 2 * BLOCK), 1) == 2 * iota((BLOCK, 2 * BLOCK), 0) + j).astype(F32).astype(BF16)
        rows.append(jnp.dot(delta, pick, preferred_element_type=F32) + iota((16, BLOCK), 1).astype(F32))
        cols.append(
            lax.dot_general(pick_t, delta, (((1,), (1,)), ((), ())), preferred_element_type=F32)
            + iota((BLOCK, 16), 0).astype(F32)
        )
    q_at = iota((BLOCK, BLOCK), 1).astype(F32)
    p_at = iota((BLOCK, BLOCK), 0).astype(F32)
    smooth, middle, degree_mid = [], None, None
    for cq in range(HALO // 2, HALO // 2 + HALO + 1):
        blocks = []
        for cp in range(cq - 2, cq + 3):
            off = float((cq - cp) * BLOCK)
            adj = jnp.zeros((BLOCK, BLOCK), F32)
            for j in range(2):
                adj += jnp.where(cols[j][:, cp : cp + 1] == q_at + off, 1.0, 0.0)
                adj += jnp.where(rows[j][cq : cq + 1, :] == p_at - off, 1.0, 0.0)
            blocks.append(adj.astype(BF16))
        adj = jnp.concatenate(blocks, axis=0)
        around = jnp.dot(window[:, (cq - 2) * BLOCK : (cq + 3) * BLOCK], adj, preferred_element_type=F32)
        degree = around[DATES : DATES + 1]
        own = window[0:DATES, cq * BLOCK : (cq + 1) * BLOCK].astype(F32)
        smooth.append(degree * own - around[0:DATES])
        if cq == HALO:
            middle, degree_mid = adj, degree
    field = jnp.concatenate(smooth, axis=1)
    high = field.astype(BF16)
    low = (field - high.astype(F32)).astype(BF16)
    around = jnp.dot(high, middle, preferred_element_type=F32) + jnp.dot(low, middle, preferred_element_type=F32)
    return 0.05 * (degree_mid * smooth[HALO // 2] - around)


def kernel(
    tiles_h, row_h, col_h, count_h, slip_h, obs_h, edge_h, resid_h, grad_ref,
    tb0, tb1, row_v, col_v, count_v, slip_v, slip_blk, ext, obs_v, edges_v,
    order_v, same_v, ends_v, order, same, ends, run_ref,
    sib_send, sib_recv, chip_sum, zl_recv, resid_v, resid_blk0, resid_blk1, curve_v,
    rs_send, rs_recv, z_send, z_recv,
    tile_sem, in_sem, edge_sem, sm_sem, out_sem,
    sib_ss, sib_rs, halo_ss, halo_rs, zl_ss, zl_rs, res_ss, res_rs, rs_ss, rs_rs, z_ss, z_rs,
):
    ps, pt = lax.axis_index("ps"), lax.axis_index("patch")
    y, zh, x = ps // 16, ps // 4 % 4, ps % 4
    core = pt % 2
    par = x % 2
    tbs = (tb0, tb1)
    resid_blks = (resid_blk0, resid_blk1)

    def at(yy, zz, xx):
        return (yy * 16 + zz * 4 + xx, pt)

    sibling = (ps, pt + 1 - 2 * core)
    across = (ps, (pt + 2) % 4)
    after = (ps, (pt + 1) % 4)
    before = (ps, (pt + 3) % 4)

    small = [
        pltpu.make_async_copy(row_h, row_v, in_sem.at[0]),
        pltpu.make_async_copy(col_h, col_v, in_sem.at[1]),
        pltpu.make_async_copy(count_h, count_v, in_sem.at[2]),
    ]
    slip_in = pltpu.make_async_copy(slip_h, slip_v, in_sem.at[3])
    for copy in small:
        copy.start()
    slip_in.start()
    tile_in = [
        pltpu.make_async_copy(tiles_h.at[pl.ds(c * CH, CH)], tbs[c], tile_sem.at[c]) for c in range(CHUNKS)
    ]
    for copy in tile_in:
        copy.start()
    obs_in = pltpu.make_async_copy(
        obs_h.at[:, pl.ds(pl.multiple_of(core * HALF, HALF), HALF)], obs_v, in_sem.at[4]
    )
    obs_in.start()
    base = pt * COLS + ps // 2
    edge_in = []
    for w in range(WIN):
        block = (base + 128 - HALO + w) % 128
        edge_in.append(
            pltpu.make_async_copy(
                edge_h.at[:, pl.ds(pl.multiple_of(block * 256, 256), 256)], edges_v.at[w], edge_sem.at[w]
            )
        )
    for copy in edge_in:
        copy.start()

    barrier = pltpu.get_barrier_semaphore()
    partners = [(ps, (pt + k) % 4) for k in (1, 2, 3)]
    partners += [at(xor(y, n), zh, xor(x, m)) for n in range(4) for m in range(4) if n or m]
    partners += [at(y, xor(zh, m), x) for m in (1, 2, 3)]
    for device in partners:
        pl.semaphore_signal(barrier, inc=1, device_id=device, device_id_type=MESH)

    for copy in small:
        copy.wait()
    sort_slots(row_v, col_v, count_v, order_v, same_v, ends_v)
    staged = [
        pltpu.make_async_copy(order_v, order, sm_sem.at[0]),
        pltpu.make_async_copy(same_v, same, sm_sem.at[1]),
        pltpu.make_async_copy(ends_v, ends, sm_sem.at[2]),
    ]
    for copy in staged:
        copy.start()
    slip_in.wait()
    for k in range(COLS):
        slip_blk[k] = slip_v[:, k * BLOCK : (k + 1) * BLOCK]
    ext[0:DATES, HALO * BLOCK : HALO * BLOCK + K_DEV] = slip_v[...]
    ext[DATES:, :] = jnp.ones((16, K_DEV + 2 * HALO * BLOCK), BF16)
    run_ref[SLOTS] = jnp.zeros((DATES, BLOCK), F32)
    for copy in staged:
        copy.wait()

    for c in range(CHUNKS):
        tile_in[c].wait()
        tile_pass(0, c, tbs[c], slip_blk, order, same, run_ref)

    pl.semaphore_wait(barrier, len(partners))

    def remote(src, dst, ss, rs, device):
        return pltpu.make_async_remote_copy(
            src_ref=src, dst_ref=dst, send_sem=ss, recv_sem=rs, device_id=device, device_id_type=MESH
        )

    sib = []
    for g, (first, dates) in enumerate(GROUPS):
        for k in range(8):
            sib_send[first : first + dates, k * BLOCK : (k + 1) * BLOCK] = gathered(
                0, (1 - core) * 8 + k, run_ref, ends, first, dates
            )
        lines = pl.ds(first, dates)
        sib.append(remote(sib_send.at[lines], sib_recv.at[lines], sib_ss.at[g], sib_rs.at[g], sibling))
        sib[g].start()
    halo = [
        remote(
            slip_v.at[:, pl.ds(K_DEV - HALO * BLOCK, HALO * BLOCK)],
            ext.at[pl.ds(0, DATES), pl.ds(0, HALO * BLOCK)],
            halo_ss.at[0], halo_rs.at[0], after,
        ),
        remote(
            slip_v.at[:, pl.ds(0, HALO * BLOCK)],
            ext.at[pl.ds(0, DATES), pl.ds(HALO * BLOCK + K_DEV, HALO * BLOCK)],
            halo_ss.at[1], halo_rs.at[1], before,
        ),
    ]
    zl = []
    for k in range(8):
        chip_sum[:, k * BLOCK : (k + 1) * BLOCK] = gathered(0, core * 8 + k, run_ref, ends, 0, DATES)
    for g, (first, dates) in enumerate(GROUPS):
        sib[g].wait_recv()
        lines = pl.ds(first, dates)
        chip_sum[lines] = chip_sum[lines] + sib_recv[lines]
        zl.append(remote(chip_sum.at[lines], zl_recv.at[lines], zl_ss.at[g], zl_rs.at[g], across))
        zl[g].start()
    for copy in halo:
        copy.start()
    obs_in.wait()
    for copy in edge_in:
        copy.wait()

    res, outs, plane = [], [], {}

    def own_half(g):
        first, dates = GROUPS[g]
        lines = pl.ds(first, dates)
        zl[g].wait_recv()
        value = chip_sum[lines] + zl_recv[lines] - obs_v[lines]
        resid_v[core, lines] = value
        res.append(
            remote(resid_v.at[core, lines], resid_v.at[core, lines], res_ss.at[g], res_rs.at[g], sibling)
        )
        res[g].start()
        for k in range(8):
            resid_blks[g][core * 8 + k] = value[:, k * BLOCK : (k + 1) * BLOCK].astype(BF16)

    def other_half(g):
        first, dates = GROUPS[g]
        res[g].wait_recv()
        value = resid_v[1 - core, pl.ds(first, dates)]
        for k in range(8):
            resid_blks[g][(1 - core) * 8 + k] = value[:, k * BLOCK : (k + 1) * BLOCK].astype(BF16)

    def to_plane(g):
        first, dates = GROUPS[g]
        lines = slice(first, first + dates)
        low = iota((dates, BLOCK), 1) < 64
        for n in (2, 1, 3, 0):
            for mb in (2, 0):
                line = xor(y, n) * 8 + xor(x, mb) // 2
                for pair in range(2):
                    b0 = gathered(1, line + 4 * pair, run_ref, ends, first, dates)
                    b1 = gathered(1, line + 4 * pair + 2, run_ref, ends, first, dates)
                    lanes = slice(pair * BLOCK, (pair + 1) * BLOCK)
                    rs_send[n * 4 + mb + par, lines, lanes] = jnp.where(low, b0, pltpu.roll(b1, 64, 1))
                    rs_send[n * 4 + mb + 1 - par, lines, lanes] = jnp.where(low, pltpu.roll(b0, 64, 1), b1)
                for m in (mb, mb + 1):
                    if n or m:
                        i = n * 4 + m
                        plane[g, i] = remote(
                            rs_send.at[i, pl.ds(first, dates)], rs_recv.at[i, pl.ds(first, dates)],
                            rs_ss.at[g, i], rs_rs.at[g, i], at(xor(y, n), zh, xor(x, m)),
                        )
                        plane[g, i].start()

    def from_plane(g):
        first, dates = GROUPS[g]
        lines = slice(first, first + dates)
        total = rs_send[0, lines]
        for i in (1, 4, 3, 12, 5, 7, 13, 15, 2, 8, 6, 9, 14, 11, 10):
            plane[g, i].wait_recv()
            total = total + rs_recv[i, lines]
        return total

    own_half(0)
    other_half(0)
    tile_pass(1, 0, tbs[0], resid_blks[0], order, same, run_ref, *GROUPS[0])
    own_half(1)
    tile_pass(1, 1, tbs[1], resid_blks[0], order, same, run_ref, *GROUPS[0])
    to_plane(0)
    other_half(1)
    for q in range(2):
        outs.append(pltpu.make_async_copy(resid_v.at[q], resid_h.at[:, pl.ds(q * HALF, HALF)], out_sem.at[q]))
        outs[q].start()
    for c in range(CHUNKS):
        tile_pass(1, c, tbs[c], resid_blks[1], order, same, run_ref, *GROUPS[1])
    to_plane(1)

    for copy in halo:
        copy.wait_recv()
    window = ext[:, pl.ds(pl.multiple_of((ps // 2) * BLOCK, BLOCK), WIN * BLOCK)]
    curve_v[...] = curvature_of(edges_v, window, base)

    total = jnp.concatenate([from_plane(0), from_plane(1)], axis=0)

    half = DATES // 2
    low_half = iota((half, BLOCK), 1) < 64

    def pack(block, odd):
        top, bottom = block[0:half], block[half:]
        if odd:
            return jnp.where(low_half, pltpu.roll(top, 64, 1), bottom)
        return jnp.where(low_half, top, pltpu.roll(bottom, 64, 1))

    for z in range(4):
        z_send[z] = pack(total[:, z // 2 * BLOCK : (z // 2 + 1) * BLOCK], z % 2)
    line = {}
    for m in (2, 1, 3):
        line[m] = remote(z_send.at[xor(zh, m)], z_recv.at[m], z_ss.at[m], z_rs.at[m], at(y, xor(zh, m), x))
        line[m].start()
    curve = curve_v[...]
    share = z_send[zh] + jnp.where(ps % 2 == 0, pack(curve, 0), pack(curve, 1))
    for m in (1, 3, 2):
        line[m].wait_recv()
        share = share + z_recv[m]
    grad_ref[0:half, :] = share[:, 0:64]
    grad_ref[half:, :] = pltpu.roll(share, 64, 1)[:, 0:64]

    for copy in outs:
        copy.wait()
    for copy in [*sib, *halo, *zl, *res, *plane.values(), *line.values()]:
        copy.wait_send()


def body(tiles, tile_row, tile_col, tile_count, slip, observations, edge_list):
    any_spec = pl.BlockSpec(memory_space=pltpu.HBM)
    vmem, dma = pltpu.VMEM, pltpu.SemaphoreType.DMA
    i32 = jnp.int32
    near = functools.partial(pltpu.with_memory_space_constraint, memory_space=pltpu.HBM)
    resid, grad = pl.pallas_call(
        kernel,
        out_shape=(
            jax.ShapeDtypeStruct((DATES, ROWS * BLOCK), F32),
            jax.ShapeDtypeStruct((DATES, 64), F32),
        ),
        in_specs=[any_spec] * 7,
        out_specs=(any_spec, pl.BlockSpec(memory_space=vmem)),
        scratch_shapes=[
            *[vmem((CH, BLOCK, BLOCK), BF16) for _ in range(CHUNKS)],
            vmem((1, 1, SLOTS), i32),
            vmem((1, 1, SLOTS), i32),
            vmem((1, 1), i32),
            vmem((DATES, K_DEV), BF16),
            vmem((COLS, DATES, BLOCK), BF16),
            vmem((DATES + 16, K_DEV + 2 * HALO * BLOCK), BF16),
            vmem((DATES, HALF), F32),
            vmem((WIN, 2, 256), i32),
            vmem((8, SLOTS), i32),
            vmem((8, SLOTS), F32),
            vmem((2 * COLS, 128), i32),
            pltpu.SMEM((8, SLOTS), i32),
            pltpu.SMEM((8, SLOTS), F32),
            pltpu.SMEM((2 * COLS, 128), i32),
            vmem((SLOTS + 1, DATES, BLOCK), F32),
            *[vmem((DATES, HALF), F32) for _ in range(4)],
            vmem((2, DATES, HALF), F32),
            *[vmem((ROWS, dates, BLOCK), BF16) for _, dates in GROUPS],
            vmem((DATES, BLOCK), F32),
            vmem((16, DATES, 256), F32),
            vmem((16, DATES, 256), F32),
            vmem((4, DATES // 2, BLOCK), F32),
            vmem((4, DATES // 2, BLOCK), F32),
            dma((CHUNKS,)), dma((5,)), dma((WIN,)), dma((3,)), dma((4,)),
            dma((2,)), dma((2,)), dma((2,)), dma((2,)), dma((2,)), dma((2,)), dma((2,)), dma((2,)),
            dma((2, 16)), dma((2, 16)), dma((4,)), dma((4,)),
        ],
        compiler_params=pltpu.CompilerParams(
            collective_id=0, has_side_effects=True, vmem_limit_bytes=48 * 2**20
        ),
        cost_estimate=pl.CostEstimate(flops=2 * 10**9, bytes_accessed=10 * 2**20, transcendentals=0),
    )(
        *(near(a) for a in (tiles[0, 0], tile_row, tile_col)),
        tile_count,
        *(near(a) for a in (slip, observations, edge_list)),
    )
    return placed(resid, grad)


def placed(resid, grad):
    def copies(resid_in, grad_in, resid_out, grad_out, sem):
        moves = [
            pltpu.make_async_copy(resid_in, resid_out, sem.at[0]),
            pltpu.make_async_copy(grad_in, grad_out, sem.at[1]),
        ]
        for move in moves:
            move.start()
        for move in moves:
            move.wait()

    return pl.pallas_call(
        copies,
        out_shape=tuple(jax.ShapeDtypeStruct(a.shape, a.dtype) for a in (resid, grad)),
        in_specs=[pl.BlockSpec(memory_space=pl.ANY)] * 2,
        out_specs=(pl.BlockSpec(memory_space=pl.ANY),) * 2,
        scratch_shapes=[pltpu.SemaphoreType.DMA((2,))],
        compiler_params=pltpu.CompilerParams(vmem_limit_bytes=2**20),
    )(resid, grad)


def solution(mesh):
    in_specs = (
        P("ps", "patch", None, None, None),
        P("ps", "patch", None),
        P("ps", "patch", None),
        P("ps", "patch"),
        P(None, "patch"),
        P(None, "ps"),
        P(),
    )
    out_specs = (P(None, "ps"), P(None, ("patch", "ps")))
    return jax.shard_map(body, mesh=mesh, in_specs=in_specs, out_specs=out_specs, check_vma=False)
```

```python
import functools

import jax
import jax.numpy as jnp
from jax import lax
from jax.experimental import pallas as pl
from jax.experimental.pallas import tpu as pltpu
from jax.sharding import PartitionSpec as P

F32 = jnp.float32
BF16 = jnp.bfloat16
MESH = pl.DeviceIdType.MESH

BLOCK = 128
DATES = 48
SLOTS = 256
CHUNKS = 2
CH = SLOTS // CHUNKS
ROWS = 16
COLS = 32
HALF = ROWS // 2 * BLOCK
K_DEV = COLS * BLOCK
HALO = 4
WIN = 2 * HALO + 1
PATCHES = 16384
UNROLL = 64
GROUPS = ((0, 16), (16, 32))


def xor(value, m):
    if m == 0:
        return value
    if m == 1:
        return value + 1 - 2 * (value % 2)
    if m == 2:
        return (value + 2) % 4
    return 3 - value


def iota(shape, dim):
    return lax.broadcasted_iota(jnp.int32, shape, dim)


def sort_slots(row_ref, col_ref, count_ref, order, same, ends):
    shape = (SLOTS, SLOTS)
    t_lane = iota((1, SLOTS), 1)
    live = t_lane < count_ref[...]
    row = row_ref[0]
    col = col_ref[0]
    chunk_f = (t_lane // CH).astype(F32)
    t_f = t_lane.astype(F32)
    diagonal = iota(shape, 0) == iota(shape, 1)
    lane_f = iota(shape, 1).astype(F32)
    which = iota((16, SLOTS), 0)
    picker = (iota((SLOTS, 128), 0) // CH == iota((SLOTS, 128), 1)).astype(BF16)
    chunk_at = iota((COLS, 128), 1)
    for n, (mine, other, dead, limit) in enumerate(((row, col, ROWS, COLS - 1), (col, row, COLS, ROWS - 1))):
        own = jnp.where(live, mine, dead).astype(F32)
        key = (chunk_f * 64.0 + own) * SLOTS + t_f
        key_col = jnp.sum(jnp.where(diagonal, key, 0.0), axis=1, keepdims=True)
        rank = jnp.sum(jnp.where(key < key_col, 1.0, 0.0), axis=1, keepdims=True)
        one_hot = jnp.where(rank == lane_f, 1.0, 0.0).astype(BF16)
        values = jnp.where(which == 0, t_f - chunk_f * CH, jnp.where(which == 1, other.astype(F32), own))
        ordered = jnp.dot(values.astype(BF16), one_hot, preferred_element_type=F32)
        order[2 * n : 2 * n + 1, :] = jnp.clip(ordered[0:1].astype(jnp.int32), 0, CH - 1)
        order[2 * n + 1 : 2 * n + 2, :] = jnp.clip(ordered[1:2].astype(jnp.int32), 0, limit)
        key_s = ordered[2:3]
        before = pltpu.roll(jnp.broadcast_to(key_s, (8, SLOTS)), 1, 1)[0:1]
        same[n : n + 1, :] = jnp.where((key_s == before) & (t_lane % CH != 0), 1.0, 0.0)
        line = iota((COLS, SLOTS), 0).astype(F32)
        upto = jnp.dot(jnp.where(own <= line, 1.0, 0.0).astype(BF16), picker, preferred_element_type=F32)
        there = jnp.dot(jnp.where(own == line, 1.0, 0.0).astype(BF16), picker, preferred_element_type=F32)
        at = chunk_at * CH + upto.astype(jnp.int32) - 1
        ends[n * COLS : (n + 1) * COLS, :] = jnp.clip(jnp.where(there > 0.5, at, SLOTS), 0, SLOTS)


def tile_pass(n, c, tiles, left, order, same, run_ref, first=0, dates=DATES):
    zeros = jnp.zeros((dates, BLOCK), BF16)
    lines = slice(first, first + dates)
    contract = (((1,), (1,)), ((), ())) if n == 0 else (((1,), (0,)), ((), ()))

    def step(g, run):
        for u in range(0, UNROLL, 2):
            s = c * CH + g * UNROLL + u
            pair = jnp.concatenate([tiles[order[2 * n, s]], tiles[order[2 * n, s + 1]]], axis=1 - n)
            lhs = jnp.concatenate(
                [
                    jnp.concatenate([left[order[2 * n + 1, s]], zeros], axis=1),
                    jnp.concatenate([zeros, left[order[2 * n + 1, s + 1]]], axis=1),
                ],
                axis=0,
            )
            prod = lax.dot_general(lhs, pair, contract, preferred_element_type=F32)
            run = prod[0:dates] + run * same[n, s]
            run_ref[s, lines] = run
            run = prod[dates:] + run * same[n, s + 1]
            run_ref[s + 1, lines] = run
        return run

    lax.fori_loop(0, CH // UNROLL, step, jnp.zeros((dates, BLOCK), F32))


def gathered(n, line, run_ref, ends, first, dates):
    lines = slice(first, first + dates)
    total = run_ref[ends[n * COLS + line, 0], lines]
    for c in range(1, CHUNKS):
        total += run_ref[ends[n * COLS + line, c], lines]
    return total


def curvature_of(edges, window, base):
    e_at = iota((WIN, 2 * BLOCK), 1)
    block_at = (iota((WIN, 2 * BLOCK), 0) + base + 128 - HALO) % 128
    anchor = block_at * BLOCK + e_at // 2
    delta = edges[:, 0, :] + edges[:, 1, :] - 2 * anchor
    delta = (delta + 3 * PATCHES // 2 + PATCHES) % PATCHES - PATCHES // 2
    delta = jnp.concatenate([delta.astype(F32), jnp.zeros((16 - WIN, 2 * BLOCK), F32)], axis=0).astype(BF16)
    rows, cols = [], []
    for j in range(2):
        pick = (iota((2 * BLOCK, BLOCK), 0) == 2 * iota((2 * BLOCK, BLOCK), 1) + j).astype(F32).astype(BF16)
        pick_t = (iota((BLOCK, 2 * BLOCK), 1) == 2 * iota((BLOCK, 2 * BLOCK), 0) + j).astype(F32).astype(BF16)
        rows.append(jnp.dot(delta, pick, preferred_element_type=F32) + iota((16, BLOCK), 1).astype(F32))
        cols.append(
            lax.dot_general(pick_t, delta, (((1,), (1,)), ((), ())), preferred_element_type=F32)
            + iota((BLOCK, 16), 0).astype(F32)
        )
    q_at = iota((BLOCK, BLOCK), 1).astype(F32)
    p_at = iota((BLOCK, BLOCK), 0).astype(F32)
    smooth, middle, degree_mid = [], None, None
    for cq in range(HALO // 2, HALO // 2 + HALO + 1):
        blocks = []
        for cp in range(cq - 2, cq + 3):
            off = float((cq - cp) * BLOCK)
            adj = jnp.zeros((BLOCK, BLOCK), F32)
            for j in range(2):
                adj += jnp.where(cols[j][:, cp : cp + 1] == q_at + off, 1.0, 0.0)
                adj += jnp.where(rows[j][cq : cq + 1, :] == p_at - off, 1.0, 0.0)
            blocks.append(adj.astype(BF16))
        adj = jnp.concatenate(blocks, axis=0)
        around = jnp.dot(window[:, (cq - 2) * BLOCK : (cq + 3) * BLOCK], adj, preferred_element_type=F32)
        degree = around[DATES : DATES + 1]
        own = window[0:DATES, cq * BLOCK : (cq + 1) * BLOCK].astype(F32)
        smooth.append(degree * own - around[0:DATES])
        if cq == HALO:
            middle, degree_mid = adj, degree
    field = jnp.concatenate(smooth, axis=1)
    high = field.astype(BF16)
    low = (field - high.astype(F32)).astype(BF16)
    around = jnp.dot(high, middle, preferred_element_type=F32) + jnp.dot(low, middle, preferred_element_type=F32)
    return 0.05 * (degree_mid * smooth[HALO // 2] - around)


def kernel(
    tiles_h, row_h, col_h, count_h, slip_h, obs_h, edge_h, resid_h, grad_ref,
    tb0, tb1, row_v, col_v, count_v, slip_v, slip_blk, ext, obs_v, edges_v,
    order_v, same_v, ends_v, order, same, ends, run_ref,
    sib_send, sib_recv, chip_sum, zl_recv, resid_v, resid_blk0, resid_blk1, curve_v,
    rs_send, rs_recv, z_send, z_recv,
    tile_sem, in_sem, edge_sem, sm_sem, out_sem,
    sib_ss, sib_rs, halo_ss, halo_rs, zl_ss, zl_rs, res_ss, res_rs, rs_ss, rs_rs, z_ss, z_rs,
):
    ps, pt = lax.axis_index("ps"), lax.axis_index("patch")
    y, zh, x = ps // 16, ps // 4 % 4, ps % 4
    core = pt % 2
    par = x % 2
    tbs = (tb0, tb1)
    resid_blks = (resid_blk0, resid_blk1)

    def at(yy, zz, xx):
        return (yy * 16 + zz * 4 + xx, pt)

    sibling = (ps, pt + 1 - 2 * core)
    across = (ps, (pt + 2) % 4)
    after = (ps, (pt + 1) % 4)
    before = (ps, (pt + 3) % 4)

    small = [
        pltpu.make_async_copy(row_h, row_v, in_sem.at[0]),
        pltpu.make_async_copy(col_h, col_v, in_sem.at[1]),
        pltpu.make_async_copy(count_h, count_v, in_sem.at[2]),
    ]
    slip_in = pltpu.make_async_copy(slip_h, slip_v, in_sem.at[3])
    for copy in small:
        copy.start()
    slip_in.start()
    tile_in = [
        pltpu.make_async_copy(tiles_h.at[pl.ds(c * CH, CH)], tbs[c], tile_sem.at[c]) for c in range(CHUNKS)
    ]
    for copy in tile_in:
        copy.start()
    obs_in = pltpu.make_async_copy(
        obs_h.at[:, pl.ds(pl.multiple_of(core * HALF, HALF), HALF)], obs_v, in_sem.at[4]
    )
    obs_in.start()
    base = pt * COLS + ps // 2
    edge_in = []
    for w in range(WIN):
        block = (base + 128 - HALO + w) % 128
        edge_in.append(
            pltpu.make_async_copy(
                edge_h.at[:, pl.ds(pl.multiple_of(block * 256, 256), 256)], edges_v.at[w], edge_sem.at[w]
            )
        )
    for copy in edge_in:
        copy.start()

    barrier = pltpu.get_barrier_semaphore()
    partners = [(ps, (pt + k) % 4) for k in (1, 2, 3)]
    partners += [at(xor(y, n), zh, xor(x, m)) for n in range(4) for m in range(4) if n or m]
    partners += [at(y, xor(zh, m), x) for m in (1, 2, 3)]
    for device in partners:
        pl.semaphore_signal(barrier, inc=1, device_id=device, device_id_type=MESH)

    for copy in small:
        copy.wait()
    sort_slots(row_v, col_v, count_v, order_v, same_v, ends_v)
    staged = [
        pltpu.make_async_copy(order_v, order, sm_sem.at[0]),
        pltpu.make_async_copy(same_v, same, sm_sem.at[1]),
        pltpu.make_async_copy(ends_v, ends, sm_sem.at[2]),
    ]
    for copy in staged:
        copy.start()
    slip_in.wait()
    for k in range(COLS):
        slip_blk[k] = slip_v[:, k * BLOCK : (k + 1) * BLOCK]
    ext[0:DATES, HALO * BLOCK : HALO * BLOCK + K_DEV] = slip_v[...]
    ext[DATES:, :] = jnp.ones((16, K_DEV + 2 * HALO * BLOCK), BF16)
    run_ref[SLOTS] = jnp.zeros((DATES, BLOCK), F32)
    for copy in staged:
        copy.wait()

    for c in range(CHUNKS):
        tile_in[c].wait()
        tile_pass(0, c, tbs[c], slip_blk, order, same, run_ref)

    pl.semaphore_wait(barrier, len(partners))

    def remote(src, dst, ss, rs, device):
        return pltpu.make_async_remote_copy(
            src_ref=src, dst_ref=dst, send_sem=ss, recv_sem=rs, device_id=device, device_id_type=MESH
        )

    sib = []
    for g, (first, dates) in enumerate(GROUPS):
        for k in range(8):
            sib_send[first : first + dates, k * BLOCK : (k + 1) * BLOCK] = gathered(
                0, (1 - core) * 8 + k, run_ref, ends, first, dates
            )
        lines = pl.ds(first, dates)
        sib.append(remote(sib_send.at[lines], sib_recv.at[lines], sib_ss.at[g], sib_rs.at[g], sibling))
        sib[g].start()
    halo = [
        remote(
            slip_v.at[:, pl.ds(K_DEV - HALO * BLOCK, HALO * BLOCK)],
            ext.at[pl.ds(0, DATES), pl.ds(0, HALO * BLOCK)],
            halo_ss.at[0], halo_rs.at[0], after,
        ),
        remote(
            slip_v.at[:, pl.ds(0, HALO * BLOCK)],
            ext.at[pl.ds(0, DATES), pl.ds(HALO * BLOCK + K_DEV, HALO * BLOCK)],
            halo_ss.at[1], halo_rs.at[1], before,
        ),
    ]
    zl = []
    for k in range(8):
        chip_sum[:, k * BLOCK : (k + 1) * BLOCK] = gathered(0, core * 8 + k, run_ref, ends, 0, DATES)
    for g, (first, dates) in enumerate(GROUPS):
        sib[g].wait_recv()
        lines = pl.ds(first, dates)
        chip_sum[lines] = chip_sum[lines] + sib_recv[lines]
        zl.append(remote(chip_sum.at[lines], zl_recv.at[lines], zl_ss.at[g], zl_rs.at[g], across))
        zl[g].start()
    for copy in halo:
        copy.start()
    obs_in.wait()
    for copy in edge_in:
        copy.wait()

    res, outs, plane = [], [], {}

    def own_half(g):
        first, dates = GROUPS[g]
        lines = pl.ds(first, dates)
        zl[g].wait_recv()
        value = chip_sum[lines] + zl_recv[lines] - obs_v[lines]
        resid_v[core, lines] = value
        res.append(
            remote(resid_v.at[core, lines], resid_v.at[core, lines], res_ss.at[g], res_rs.at[g], sibling)
        )
        res[g].start()
        for k in range(8):
            resid_blks[g][core * 8 + k] = value[:, k * BLOCK : (k + 1) * BLOCK].astype(BF16)

    def other_half(g):
        first, dates = GROUPS[g]
        res[g].wait_recv()
        value = resid_v[1 - core, pl.ds(first, dates)]
        for k in range(8):
            resid_blks[g][(1 - core) * 8 + k] = value[:, k * BLOCK : (k + 1) * BLOCK].astype(BF16)

    def to_plane(g, part, pairs):
        first, dates = GROUPS[g]
        lines = slice(first, first + dates)
        low = iota((dates, BLOCK), 1) < 64
        lanes_sent = pl.ds(pairs[0] * BLOCK, len(pairs) * BLOCK)
        for n in (2, 1, 3, 0):
            for mb in (2, 0):
                line = xor(y, n) * 8 + xor(x, mb) // 2
                for pair in pairs:
                    b0 = gathered(1, line + 4 * pair, run_ref, ends, first, dates)
                    b1 = gathered(1, line + 4 * pair + 2, run_ref, ends, first, dates)
                    lanes = slice(pair * BLOCK, (pair + 1) * BLOCK)
                    rs_send[n * 4 + mb + par, lines, lanes] = jnp.where(low, b0, pltpu.roll(b1, 64, 1))
                    rs_send[n * 4 + mb + 1 - par, lines, lanes] = jnp.where(low, pltpu.roll(b0, 64, 1), b1)
                for m in (mb, mb + 1):
                    if n or m:
                        i = n * 4 + m
                        plane[part, i] = remote(
                            rs_send.at[i, pl.ds(first, dates), lanes_sent],
                            rs_recv.at[i, pl.ds(first, dates), lanes_sent],
                            rs_ss.at[part, i], rs_rs.at[part, i], at(xor(y, n), zh, xor(x, m)),
                        )
                        plane[part, i].start()

    def from_plane(g, part, pairs):
        first, dates = GROUPS[g]
        lines = slice(first, first + dates)
        lanes = slice(pairs[0] * BLOCK, (pairs[-1] + 1) * BLOCK)
        total = rs_send[0, lines, lanes]
        for i in (1, 4, 3, 12, 5, 7, 13, 15, 2, 8, 6, 9, 14, 11, 10):
            plane[part, i].wait_recv()
            total = total + rs_recv[i, lines, lanes]
        return total

    own_half(0)
    other_half(0)
    tile_pass(1, 0, tbs[0], resid_blks[0], order, same, run_ref, *GROUPS[0])
    own_half(1)
    tile_pass(1, 1, tbs[1], resid_blks[0], order, same, run_ref, *GROUPS[0])
    to_plane(0, 0, (0, 1))
    other_half(1)
    for q in range(2):
        outs.append(pltpu.make_async_copy(resid_v.at[q], resid_h.at[:, pl.ds(q * HALF, HALF)], out_sem.at[q]))
        outs[q].start()
    for c in range(CHUNKS):
        tile_pass(1, c, tbs[c], resid_blks[1], order, same, run_ref, *GROUPS[1])
    to_plane(1, 1, (0,))
    to_plane(1, 2, (1,))

    for copy in halo:
        copy.wait_recv()
    window = ext[:, pl.ds(pl.multiple_of((ps // 2) * BLOCK, BLOCK), WIN * BLOCK)]
    curve_v[...] = curvature_of(edges_v, window, base)

    total = from_plane(0, 0, (0, 1))
    half = DATES // 2
    low_half = iota((half, BLOCK), 1) < 64

    def pack(block, odd):
        top, bottom = block[0:half], block[half:]
        if odd:
            return jnp.where(low_half, pltpu.roll(top, 64, 1), bottom)
        return jnp.where(low_half, top, pltpu.roll(bottom, 64, 1))

    line = {}
    for m in (1, 2, 3):
        line[m] = remote(z_send.at[xor(zh, m)], z_recv.at[m], z_ss.at[m], z_rs.at[m], at(y, xor(zh, m), x))

    for pair in range(2):
        block = jnp.concatenate(
            [total[:, pair * BLOCK : (pair + 1) * BLOCK], from_plane(1, 1 + pair, (pair,))], axis=0
        )
        for odd in range(2):
            z_send[2 * pair + odd] = pack(block, odd)

        @pl.when(zh // 2 == pair)
        def near_by():
            line[1].start()

        @pl.when(zh // 2 != pair)
        def far():
            line[2].start()
            line[3].start()

    curve = curve_v[...]
    share = z_send[zh] + jnp.where(ps % 2 == 0, pack(curve, 0), pack(curve, 1))
    for m in (1, 3, 2):
        line[m].wait_recv()
        share = share + z_recv[m]
    grad_ref[0:half, :] = share[:, 0:64]
    grad_ref[half:, :] = pltpu.roll(share, 64, 1)[:, 0:64]

    for copy in outs:
        copy.wait()
    for copy in [*sib, *halo, *zl, *res, *plane.values(), *line.values()]:
        copy.wait_send()


def body(tiles, tile_row, tile_col, tile_count, slip, observations, edge_list):
    any_spec = pl.BlockSpec(memory_space=pltpu.HBM)
    vmem, dma = pltpu.VMEM, pltpu.SemaphoreType.DMA
    i32 = jnp.int32
    near = functools.partial(pltpu.with_memory_space_constraint, memory_space=pltpu.HBM)
    resid, grad = pl.pallas_call(
        kernel,
        out_shape=(
            jax.ShapeDtypeStruct((DATES, ROWS * BLOCK), F32),
            jax.ShapeDtypeStruct((DATES, 64), F32),
        ),
        in_specs=[any_spec] * 7,
        out_specs=(any_spec, pl.BlockSpec(memory_space=vmem)),
        scratch_shapes=[
            *[vmem((CH, BLOCK, BLOCK), BF16) for _ in range(CHUNKS)],
            vmem((1, 1, SLOTS), i32),
            vmem((1, 1, SLOTS), i32),
            vmem((1, 1), i32),
            vmem((DATES, K_DEV), BF16),
            vmem((COLS, DATES, BLOCK), BF16),
            vmem((DATES + 16, K_DEV + 2 * HALO * BLOCK), BF16),
            vmem((DATES, HALF), F32),
            vmem((WIN, 2, 256), i32),
            vmem((8, SLOTS), i32),
            vmem((8, SLOTS), F32),
            vmem((2 * COLS, 128), i32),
            pltpu.SMEM((8, SLOTS), i32),
            pltpu.SMEM((8, SLOTS), F32),
            pltpu.SMEM((2 * COLS, 128), i32),
            vmem((SLOTS + 1, DATES, BLOCK), F32),
            *[vmem((DATES, HALF), F32) for _ in range(4)],
            vmem((2, DATES, HALF), F32),
            *[vmem((ROWS, dates, BLOCK), BF16) for _, dates in GROUPS],
            vmem((DATES, BLOCK), F32),
            vmem((16, DATES, 256), F32),
            vmem((16, DATES, 256), F32),
            vmem((4, DATES // 2, BLOCK), F32),
            vmem((4, DATES // 2, BLOCK), F32),
            dma((CHUNKS,)), dma((5,)), dma((WIN,)), dma((3,)), dma((4,)),
            dma((2,)), dma((2,)), dma((2,)), dma((2,)), dma((2,)), dma((2,)), dma((2,)), dma((2,)),
            dma((3, 16)), dma((3, 16)), dma((4,)), dma((4,)),
        ],
        compiler_params=pltpu.CompilerParams(
            collective_id=0, has_side_effects=True, vmem_limit_bytes=48 * 2**20
        ),
        cost_estimate=pl.CostEstimate(flops=2 * 10**9, bytes_accessed=10 * 2**20, transcendentals=0),
    )(
        *(near(a) for a in (tiles[0, 0], tile_row, tile_col)),
        tile_count,
        *(near(a) for a in (slip, observations, edge_list)),
    )
    return placed(resid, grad)


def placed(resid, grad):
    def copies(resid_in, grad_in, resid_out, grad_out, sem):
        moves = [
            pltpu.make_async_copy(resid_in, resid_out, sem.at[0]),
            pltpu.make_async_copy(grad_in, grad_out, sem.at[1]),
        ]
        for move in moves:
            move.start()
        for move in moves:
            move.wait()

    return pl.pallas_call(
        copies,
        out_shape=tuple(jax.ShapeDtypeStruct(a.shape, a.dtype) for a in (resid, grad)),
        in_specs=[pl.BlockSpec(memory_space=pl.ANY)] * 2,
        out_specs=(pl.BlockSpec(memory_space=pl.ANY),) * 2,
        scratch_shapes=[pltpu.SemaphoreType.DMA((2,))],
        compiler_params=pltpu.CompilerParams(vmem_limit_bytes=2**20),
    )(resid, grad)


def solution(mesh):
    in_specs = (
        P("ps", "patch", None, None, None),
        P("ps", "patch", None),
        P("ps", "patch", None),
        P("ps", "patch"),
        P(None, "patch"),
        P(None, "ps"),
        P(),
    )
    out_specs = (P(None, "ps"), P(None, ("patch", "ps")))
    return jax.shard_map(body, mesh=mesh, in_specs=in_specs, out_specs=out_specs, check_vma=False)
```

```python
import functools

import jax
import jax.numpy as jnp
from jax import lax
from jax.experimental import pallas as pl
from jax.experimental.pallas import tpu as pltpu
from jax.sharding import PartitionSpec as P

F32 = jnp.float32
BF16 = jnp.bfloat16
MESH = pl.DeviceIdType.MESH

BLOCK = 128
DATES = 48
SLOTS = 256
CHUNKS = 2
CH = SLOTS // CHUNKS
ROWS = 16
COLS = 32
HALF = ROWS // 2 * BLOCK
K_DEV = COLS * BLOCK
HALO = 4
WIN = 2 * HALO + 1
PATCHES = 16384
UNROLL = 64
GROUPS = ((0, 16), (16, 32))


def xor(value, m):
    if m == 0:
        return value
    if m == 1:
        return value + 1 - 2 * (value % 2)
    if m == 2:
        return (value + 2) % 4
    return 3 - value


def iota(shape, dim):
    return lax.broadcasted_iota(jnp.int32, shape, dim)


def sort_slots(n, row_ref, col_ref, count_ref, order, same, ends):
    shape = (SLOTS, SLOTS)
    t_lane = iota((1, SLOTS), 1)
    live = t_lane < count_ref[...]
    row = row_ref[0]
    col = col_ref[0]
    chunk_f = (t_lane // CH).astype(F32)
    t_f = t_lane.astype(F32)
    diagonal = iota(shape, 0) == iota(shape, 1)
    lane_f = iota(shape, 1).astype(F32)
    which = iota((16, SLOTS), 0)
    picker = (iota((SLOTS, 128), 0) // CH == iota((SLOTS, 128), 1)).astype(BF16)
    chunk_at = iota((COLS, 128), 1)
    mine, other, dead, limit = ((row, col, ROWS, COLS - 1), (col, row, COLS, ROWS - 1))[n]
    own = jnp.where(live, mine, dead).astype(F32)
    key = (chunk_f * 64.0 + own) * SLOTS + t_f
    key_col = jnp.sum(jnp.where(diagonal, key, 0.0), axis=1, keepdims=True)
    rank = jnp.sum(jnp.where(key < key_col, 1.0, 0.0), axis=1, keepdims=True)
    one_hot = jnp.where(rank == lane_f, 1.0, 0.0).astype(BF16)
    values = jnp.where(which == 0, t_f - chunk_f * CH, jnp.where(which == 1, other.astype(F32), own))
    ordered = jnp.dot(values.astype(BF16), one_hot, preferred_element_type=F32)
    order[0:1, :] = jnp.clip(ordered[0:1].astype(jnp.int32), 0, CH - 1)
    order[1:2, :] = jnp.clip(ordered[1:2].astype(jnp.int32), 0, limit)
    key_s = ordered[2:3]
    before = pltpu.roll(jnp.broadcast_to(key_s, (8, SLOTS)), 1, 1)[0:1]
    same[0:1, :] = jnp.where((key_s == before) & (t_lane % CH != 0), 1.0, 0.0)
    line = iota((COLS, SLOTS), 0).astype(F32)
    upto = jnp.dot(jnp.where(own <= line, 1.0, 0.0).astype(BF16), picker, preferred_element_type=F32)
    there = jnp.dot(jnp.where(own == line, 1.0, 0.0).astype(BF16), picker, preferred_element_type=F32)
    at = chunk_at * CH + upto.astype(jnp.int32) - 1
    ends[...] = jnp.clip(jnp.where(there > 0.5, at, SLOTS), 0, SLOTS)


def tile_pass(n, c, tiles, left, order, same, run_ref, first=0, dates=DATES):
    zeros = jnp.zeros((dates, BLOCK), BF16)
    lines = slice(first, first + dates)
    contract = (((1,), (1,)), ((), ())) if n == 0 else (((1,), (0,)), ((), ()))

    def step(g, run):
        for u in range(0, UNROLL, 2):
            s = c * CH + g * UNROLL + u
            pair = jnp.concatenate([tiles[order[0, s]], tiles[order[0, s + 1]]], axis=1 - n)
            lhs = jnp.concatenate(
                [
                    jnp.concatenate([left[order[1, s]], zeros], axis=1),
                    jnp.concatenate([zeros, left[order[1, s + 1]]], axis=1),
                ],
                axis=0,
            )
            prod = lax.dot_general(lhs, pair, contract, preferred_element_type=F32)
            run = prod[0:dates] + run * same[0, s]
            run_ref[s, lines] = run
            run = prod[dates:] + run * same[0, s + 1]
            run_ref[s + 1, lines] = run
        return run

    lax.fori_loop(0, CH // UNROLL, step, jnp.zeros((dates, BLOCK), F32))


def gathered(line, run_ref, ends, first, dates):
    lines = slice(first, first + dates)
    total = run_ref[ends[line, 0], lines]
    for c in range(1, CHUNKS):
        total += run_ref[ends[line, c], lines]
    return total


def curvature_of(edges, window, base):
    e_at = iota((WIN, 2 * BLOCK), 1)
    block_at = (iota((WIN, 2 * BLOCK), 0) + base + 128 - HALO) % 128
    anchor = block_at * BLOCK + e_at // 2
    delta = edges[:, 0, :] + edges[:, 1, :] - 2 * anchor
    delta = (delta + 3 * PATCHES // 2 + PATCHES) % PATCHES - PATCHES // 2
    delta = jnp.concatenate([delta.astype(F32), jnp.zeros((16 - WIN, 2 * BLOCK), F32)], axis=0).astype(BF16)
    rows, cols = [], []
    for j in range(2):
        pick = (iota((2 * BLOCK, BLOCK), 0) == 2 * iota((2 * BLOCK, BLOCK), 1) + j).astype(F32).astype(BF16)
        pick_t = (iota((BLOCK, 2 * BLOCK), 1) == 2 * iota((BLOCK, 2 * BLOCK), 0) + j).astype(F32).astype(BF16)
        rows.append(jnp.dot(delta, pick, preferred_element_type=F32) + iota((16, BLOCK), 1).astype(F32))
        cols.append(
            lax.dot_general(pick_t, delta, (((1,), (1,)), ((), ())), preferred_element_type=F32)
            + iota((BLOCK, 16), 0).astype(F32)
        )
    q_at = iota((BLOCK, BLOCK), 1).astype(F32)
    p_at = iota((BLOCK, BLOCK), 0).astype(F32)
    smooth, middle, degree_mid = [], None, None
    for cq in range(HALO // 2, HALO // 2 + HALO + 1):
        blocks = []
        for cp in range(cq - 2, cq + 3):
            off = float((cq - cp) * BLOCK)
            adj = jnp.zeros((BLOCK, BLOCK), F32)
            for j in range(2):
                adj += jnp.where(cols[j][:, cp : cp + 1] == q_at + off, 1.0, 0.0)
                adj += jnp.where(rows[j][cq : cq + 1, :] == p_at - off, 1.0, 0.0)
            blocks.append(adj.astype(BF16))
        adj = jnp.concatenate(blocks, axis=0)
        around = jnp.dot(window[:, (cq - 2) * BLOCK : (cq + 3) * BLOCK], adj, preferred_element_type=F32)
        degree = around[DATES : DATES + 1]
        own = window[0:DATES, cq * BLOCK : (cq + 1) * BLOCK].astype(F32)
        smooth.append(degree * own - around[0:DATES])
        if cq == HALO:
            middle, degree_mid = adj, degree
    field = jnp.concatenate(smooth, axis=1)
    high = field.astype(BF16)
    low = (field - high.astype(F32)).astype(BF16)
    around = jnp.dot(high, middle, preferred_element_type=F32) + jnp.dot(low, middle, preferred_element_type=F32)
    return 0.05 * (degree_mid * smooth[HALO // 2] - around)


def kernel(
    tiles_h, row_h, col_h, count_h, slip_h, obs_h, edge_h, resid_h, grad_ref,
    tb0, tb1, row_v, col_v, count_v, slip_v, slip_blk, ext, obs_v, edges_v,
    order_v0, same_v0, ends_v0, order_v1, same_v1, ends_v1, order0, same0, ends0, order1, same1, ends1, run_ref,
    sib_send, sib_recv, chip_sum, zl_recv, resid_v, resid_blk0, resid_blk1, curve_v,
    rs_send, rs_recv, z_send, z_recv,
    tile_sem, in_sem, edge_sem, sm_sem, out_sem,
    sib_ss, sib_rs, halo_ss, halo_rs, zl_ss, zl_rs, res_ss, res_rs, rs_ss, rs_rs, z_ss, z_rs,
):
    ps, pt = lax.axis_index("ps"), lax.axis_index("patch")
    y, zh, x = ps // 16, ps // 4 % 4, ps % 4
    core = pt % 2
    par = x % 2
    tbs = (tb0, tb1)
    tables_v = ((order_v0, same_v0, ends_v0), (order_v1, same_v1, ends_v1))
    tables = ((order0, same0, ends0), (order1, same1, ends1))
    order, same, ends = zip(*tables)
    resid_blks = (resid_blk0, resid_blk1)

    def at(yy, zz, xx):
        return (yy * 16 + zz * 4 + xx, pt)

    sibling = (ps, pt + 1 - 2 * core)
    across = (ps, (pt + 2) % 4)
    after = (ps, (pt + 1) % 4)
    before = (ps, (pt + 3) % 4)

    small = [
        pltpu.make_async_copy(row_h, row_v, in_sem.at[0]),
        pltpu.make_async_copy(col_h, col_v, in_sem.at[1]),
        pltpu.make_async_copy(count_h, count_v, in_sem.at[2]),
    ]
    slip_in = pltpu.make_async_copy(slip_h, slip_v, in_sem.at[3])
    for copy in small:
        copy.start()
    slip_in.start()
    tile_in = [
        pltpu.make_async_copy(tiles_h.at[pl.ds(c * CH, CH)], tbs[c], tile_sem.at[c]) for c in range(CHUNKS)
    ]
    for copy in tile_in:
        copy.start()
    obs_in = pltpu.make_async_copy(
        obs_h.at[:, pl.ds(pl.multiple_of(core * HALF, HALF), HALF)], obs_v, in_sem.at[4]
    )
    obs_in.start()
    base = pt * COLS + ps // 2
    edge_in = []
    for w in range(WIN):
        block = (base + 128 - HALO + w) % 128
        edge_in.append(
            pltpu.make_async_copy(
                edge_h.at[:, pl.ds(pl.multiple_of(block * 256, 256), 256)], edges_v.at[w], edge_sem.at[w]
            )
        )
    for copy in edge_in:
        copy.start()

    barrier = pltpu.get_barrier_semaphore()
    partners = [(ps, (pt + k) % 4) for k in (1, 2, 3)]
    partners += [at(xor(y, n), zh, xor(x, m)) for n in range(4) for m in range(4) if n or m]
    partners += [at(y, xor(zh, m), x) for m in (1, 2, 3)]
    for device in partners:
        pl.semaphore_signal(barrier, inc=1, device_id=device, device_id_type=MESH)

    for copy in small:
        copy.wait()

    def sort_by(n):
        sort_slots(n, row_v, col_v, count_v, *tables_v[n])
        staged = [
            pltpu.make_async_copy(here, there, sm_sem.at[3 * n + i])
            for i, (here, there) in enumerate(zip(tables_v[n], tables[n], strict=True))
        ]
        for copy in staged:
            copy.start()
        return staged

    staged = sort_by(0)
    slip_in.wait()
    for k in range(COLS):
        slip_blk[k] = slip_v[:, k * BLOCK : (k + 1) * BLOCK]
    run_ref[SLOTS] = jnp.zeros((DATES, BLOCK), F32)
    for copy in staged:
        copy.wait()

    for c in range(CHUNKS):
        tile_in[c].wait()
        tile_pass(0, c, tbs[c], slip_blk, order[0], same[0], run_ref)

    pl.semaphore_wait(barrier, len(partners))

    def remote(src, dst, ss, rs, device):
        return pltpu.make_async_remote_copy(
            src_ref=src, dst_ref=dst, send_sem=ss, recv_sem=rs, device_id=device, device_id_type=MESH
        )

    sib = []
    for g, (first, dates) in enumerate(GROUPS):
        for k in range(8):
            sib_send[first : first + dates, k * BLOCK : (k + 1) * BLOCK] = gathered(
                (1 - core) * 8 + k, run_ref, ends[0], first, dates
            )
        lines = pl.ds(first, dates)
        sib.append(remote(sib_send.at[lines], sib_recv.at[lines], sib_ss.at[g], sib_rs.at[g], sibling))
        sib[g].start()
    halo = [
        remote(
            slip_v.at[:, pl.ds(K_DEV - HALO * BLOCK, HALO * BLOCK)],
            ext.at[pl.ds(0, DATES), pl.ds(0, HALO * BLOCK)],
            halo_ss.at[0], halo_rs.at[0], after,
        ),
        remote(
            slip_v.at[:, pl.ds(0, HALO * BLOCK)],
            ext.at[pl.ds(0, DATES), pl.ds(HALO * BLOCK + K_DEV, HALO * BLOCK)],
            halo_ss.at[1], halo_rs.at[1], before,
        ),
    ]
    zl = []
    for k in range(8):
        chip_sum[:, k * BLOCK : (k + 1) * BLOCK] = gathered(core * 8 + k, run_ref, ends[0], 0, DATES)
    for g, (first, dates) in enumerate(GROUPS):
        sib[g].wait_recv()
        lines = pl.ds(first, dates)
        chip_sum[lines] = chip_sum[lines] + sib_recv[lines]
        zl.append(remote(chip_sum.at[lines], zl_recv.at[lines], zl_ss.at[g], zl_rs.at[g], across))
        zl[g].start()
    for copy in halo:
        copy.start()
    staged = sort_by(1)
    ext[0:DATES, HALO * BLOCK : HALO * BLOCK + K_DEV] = slip_v[...]
    ext[DATES:, :] = jnp.ones((16, K_DEV + 2 * HALO * BLOCK), BF16)
    obs_in.wait()
    for copy in edge_in:
        copy.wait()
    for copy in staged:
        copy.wait()

    res, outs, plane = [], [], {}

    def own_half(g):
        first, dates = GROUPS[g]
        lines = pl.ds(first, dates)
        zl[g].wait_recv()
        value = chip_sum[lines] + zl_recv[lines] - obs_v[lines]
        resid_v[core, lines] = value
        res.append(
            remote(resid_v.at[core, lines], resid_v.at[core, lines], res_ss.at[g], res_rs.at[g], sibling)
        )
        res[g].start()
        for k in range(8):
            resid_blks[g][core * 8 + k] = value[:, k * BLOCK : (k + 1) * BLOCK].astype(BF16)

    def other_half(g):
        first, dates = GROUPS[g]
        res[g].wait_recv()
        value = resid_v[1 - core, pl.ds(first, dates)]
        for k in range(8):
            resid_blks[g][(1 - core) * 8 + k] = value[:, k * BLOCK : (k + 1) * BLOCK].astype(BF16)

    def to_plane(g, part, pairs):
        first, dates = GROUPS[g]
        lines = slice(first, first + dates)
        low = iota((dates, BLOCK), 1) < 64
        lanes_sent = pl.ds(pairs[0] * BLOCK, len(pairs) * BLOCK)
        for n in (2, 1, 3, 0):
            for mb in (2, 0):
                line = xor(y, n) * 8 + xor(x, mb) // 2
                for pair in pairs:
                    b0 = gathered(line + 4 * pair, run_ref, ends[1], first, dates)
                    b1 = gathered(line + 4 * pair + 2, run_ref, ends[1], first, dates)
                    lanes = slice(pair * BLOCK, (pair + 1) * BLOCK)
                    rs_send[n * 4 + mb + par, lines, lanes] = jnp.where(low, b0, pltpu.roll(b1, 64, 1))
                    rs_send[n * 4 + mb + 1 - par, lines, lanes] = jnp.where(low, pltpu.roll(b0, 64, 1), b1)
                for m in (mb, mb + 1):
                    if n or m:
                        i = n * 4 + m
                        plane[part, i] = remote(
                            rs_send.at[i, pl.ds(first, dates), lanes_sent],
                            rs_recv.at[i, pl.ds(first, dates), lanes_sent],
                            rs_ss.at[part, i], rs_rs.at[part, i], at(xor(y, n), zh, xor(x, m)),
                        )
                        plane[part, i].start()

    def from_plane(g, part, pairs):
        first, dates = GROUPS[g]
        lines = slice(first, first + dates)
        lanes = slice(pairs[0] * BLOCK, (pairs[-1] + 1) * BLOCK)
        total = rs_send[0, lines, lanes]
        for i in (1, 4, 3, 12, 5, 7, 13, 15, 2, 8, 6, 9, 14, 11, 10):
            plane[part, i].wait_recv()
            total = total + rs_recv[i, lines, lanes]
        return total

    own_half(0)
    other_half(0)
    tile_pass(1, 0, tbs[0], resid_blks[0], order[1], same[1], run_ref, *GROUPS[0])
    own_half(1)
    tile_pass(1, 1, tbs[1], resid_blks[0], order[1], same[1], run_ref, *GROUPS[0])
    to_plane(0, 0, (0, 1))
    other_half(1)
    for q in range(2):
        outs.append(pltpu.make_async_copy(resid_v.at[q], resid_h.at[:, pl.ds(q * HALF, HALF)], out_sem.at[q]))
        outs[q].start()
    for c in range(CHUNKS):
        tile_pass(1, c, tbs[c], resid_blks[1], order[1], same[1], run_ref, *GROUPS[1])
    to_plane(1, 1, (0,))
    to_plane(1, 2, (1,))

    for copy in halo:
        copy.wait_recv()
    window = ext[:, pl.ds(pl.multiple_of((ps // 2) * BLOCK, BLOCK), WIN * BLOCK)]
    curve_v[...] = curvature_of(edges_v, window, base)

    total = from_plane(0, 0, (0, 1))
    half = DATES // 2
    low_half = iota((half, BLOCK), 1) < 64

    def pack(block, odd):
        top, bottom = block[0:half], block[half:]
        if odd:
            return jnp.where(low_half, pltpu.roll(top, 64, 1), bottom)
        return jnp.where(low_half, top, pltpu.roll(bottom, 64, 1))

    line = {}
    for m in (1, 2, 3):
        line[m] = remote(z_send.at[xor(zh, m)], z_recv.at[m], z_ss.at[m], z_rs.at[m], at(y, xor(zh, m), x))

    for pair in range(2):
        block = jnp.concatenate(
            [total[:, pair * BLOCK : (pair + 1) * BLOCK], from_plane(1, 1 + pair, (pair,))], axis=0
        )
        for odd in range(2):
            z_send[2 * pair + odd] = pack(block, odd)

        @pl.when(zh // 2 == pair)
        def near_by():
            line[1].start()

        @pl.when(zh // 2 != pair)
        def far():
            line[2].start()
            line[3].start()

    for copy in outs:
        copy.wait()
    for copy in [*sib, *halo, *zl, *res, *plane.values()]:
        copy.wait_send()
    curve = curve_v[...]
    share = z_send[zh] + jnp.where(ps % 2 == 0, pack(curve, 0), pack(curve, 1))
    for m in (1, 3, 2):
        line[m].wait_recv()
        share = share + z_recv[m]
    grad_ref[0:half, :] = share[:, 0:64]
    grad_ref[half:, :] = pltpu.roll(share, 64, 1)[:, 0:64]

    for copy in line.values():
        copy.wait_send()


def body(tiles, tile_row, tile_col, tile_count, slip, observations, edge_list):
    any_spec = pl.BlockSpec(memory_space=pltpu.HBM)
    vmem, dma = pltpu.VMEM, pltpu.SemaphoreType.DMA
    i32 = jnp.int32
    near = functools.partial(pltpu.with_memory_space_constraint, memory_space=pltpu.HBM)
    resid, grad = pl.pallas_call(
        kernel,
        out_shape=(
            jax.ShapeDtypeStruct((DATES, ROWS * BLOCK), F32),
            jax.ShapeDtypeStruct((DATES, 64), F32),
        ),
        in_specs=[any_spec] * 7,
        out_specs=(any_spec, pl.BlockSpec(memory_space=vmem)),
        scratch_shapes=[
            *[vmem((CH, BLOCK, BLOCK), BF16) for _ in range(CHUNKS)],
            vmem((1, 1, SLOTS), i32),
            vmem((1, 1, SLOTS), i32),
            vmem((1, 1), i32),
            vmem((DATES, K_DEV), BF16),
            vmem((COLS, DATES, BLOCK), BF16),
            vmem((DATES + 16, K_DEV + 2 * HALO * BLOCK), BF16),
            vmem((DATES, HALF), F32),
            vmem((WIN, 2, 256), i32),
            *[vmem((8, SLOTS), i32), vmem((8, SLOTS), F32), vmem((COLS, 128), i32)] * 2,
            *[pltpu.SMEM((8, SLOTS), i32), pltpu.SMEM((8, SLOTS), F32), pltpu.SMEM((COLS, 128), i32)] * 2,
            vmem((SLOTS + 1, DATES, BLOCK), F32),
            *[vmem((DATES, HALF), F32) for _ in range(4)],
            vmem((2, DATES, HALF), F32),
            *[vmem((ROWS, dates, BLOCK), BF16) for _, dates in GROUPS],
            vmem((DATES, BLOCK), F32),
            vmem((16, DATES, 256), F32),
            vmem((16, DATES, 256), F32),
            vmem((4, DATES // 2, BLOCK), F32),
            vmem((4, DATES // 2, BLOCK), F32),
            dma((CHUNKS,)), dma((5,)), dma((WIN,)), dma((6,)), dma((2,)),
            dma((2,)), dma((2,)), dma((2,)), dma((2,)), dma((2,)), dma((2,)), dma((2,)), dma((2,)),
            dma((3, 16)), dma((3, 16)), dma((4,)), dma((4,)),
        ],
        compiler_params=pltpu.CompilerParams(
            collective_id=0, has_side_effects=True, vmem_limit_bytes=48 * 2**20
        ),
        cost_estimate=pl.CostEstimate(flops=2 * 10**9, bytes_accessed=10 * 2**20, transcendentals=0),
    )(
        *(near(a) for a in (tiles[0, 0], tile_row, tile_col)),
        tile_count,
        *(near(a) for a in (slip, observations, edge_list)),
    )
    return placed(resid, grad)


def placed(resid, grad):
    def copies(resid_in, grad_in, resid_out, grad_out, sem):
        moves = [
            pltpu.make_async_copy(resid_in, resid_out, sem.at[0]),
            pltpu.make_async_copy(grad_in, grad_out, sem.at[1]),
        ]
        for move in moves:
            move.start()
        for move in moves:
            move.wait()

    return pl.pallas_call(
        copies,
        out_shape=tuple(jax.ShapeDtypeStruct(a.shape, a.dtype) for a in (resid, grad)),
        in_specs=[pl.BlockSpec(memory_space=pl.ANY)] * 2,
        out_specs=(pl.BlockSpec(memory_space=pl.ANY),) * 2,
        scratch_shapes=[pltpu.SemaphoreType.DMA((2,))],
        compiler_params=pltpu.CompilerParams(vmem_limit_bytes=2**20),
    )(resid, grad)


def solution(mesh):
    in_specs = (
        P("ps", "patch", None, None, None),
        P("ps", "patch", None),
        P("ps", "patch", None),
        P("ps", "patch"),
        P(None, "patch"),
        P(None, "ps"),
        P(),
    )
    out_specs = (P(None, "ps"), P(None, ("patch", "ps")))
    return jax.shard_map(body, mesh=mesh, in_specs=in_specs, out_specs=out_specs, check_vma=False)
```

```python
import functools

import jax
import jax.numpy as jnp
from jax import lax
from jax.experimental import pallas as pl
from jax.experimental.pallas import tpu as pltpu
from jax.sharding import PartitionSpec as P

F32 = jnp.float32
BF16 = jnp.bfloat16
MESH = pl.DeviceIdType.MESH

BLOCK = 128
DATES = 48
SLOTS = 256
CHUNKS = 2
CH = SLOTS // CHUNKS
ROWS = 16
COLS = 32
HALF = ROWS // 2 * BLOCK
K_DEV = COLS * BLOCK
HALO = 4
WIN = 2 * HALO + 1
PATCHES = 16384
UNROLL = 128
GROUPS = ((0, 16), (16, 32))


def xor(value, m):
    if m == 0:
        return value
    if m == 1:
        return value + 1 - 2 * (value % 2)
    if m == 2:
        return (value + 2) % 4
    return 3 - value


def iota(shape, dim):
    return lax.broadcasted_iota(jnp.int32, shape, dim)


def sort_slots(n, row_ref, col_ref, count_ref, order, same, ends):
    shape = (SLOTS, SLOTS)
    t_lane = iota((1, SLOTS), 1)
    live = t_lane < count_ref[...]
    row = row_ref[0]
    col = col_ref[0]
    chunk_f = (t_lane // CH).astype(F32)
    t_f = t_lane.astype(F32)
    diagonal = iota(shape, 0) == iota(shape, 1)
    lane_f = iota(shape, 1).astype(F32)
    which = iota((16, SLOTS), 0)
    picker = (iota((SLOTS, 128), 0) // CH == iota((SLOTS, 128), 1)).astype(BF16)
    chunk_at = iota((COLS, 128), 1)
    mine, other, dead, limit = ((row, col, ROWS, COLS - 1), (col, row, COLS, ROWS - 1))[n]
    own = jnp.where(live, mine, dead).astype(F32)
    key = (chunk_f * 64.0 + own) * SLOTS + t_f
    key_col = jnp.sum(jnp.where(diagonal, key, 0.0), axis=1, keepdims=True)
    rank = jnp.sum(jnp.where(key < key_col, 1.0, 0.0), axis=1, keepdims=True)
    one_hot = jnp.where(rank == lane_f, 1.0, 0.0).astype(BF16)
    values = jnp.where(which == 0, t_f - chunk_f * CH, jnp.where(which == 1, other.astype(F32), own))
    ordered = jnp.dot(values.astype(BF16), one_hot, preferred_element_type=F32)
    order[0:1, :] = jnp.clip(ordered[0:1].astype(jnp.int32), 0, CH - 1)
    order[1:2, :] = jnp.clip(ordered[1:2].astype(jnp.int32), 0, limit)
    key_s = ordered[2:3]
    before = pltpu.roll(jnp.broadcast_to(key_s, (8, SLOTS)), 1, 1)[0:1]
    same[0:1, :] = jnp.where((key_s == before) & (t_lane % CH != 0), 1.0, 0.0)
    line = iota((COLS, SLOTS), 0).astype(F32)
    upto = jnp.dot(jnp.where(own <= line, 1.0, 0.0).astype(BF16), picker, preferred_element_type=F32)
    there = jnp.dot(jnp.where(own == line, 1.0, 0.0).astype(BF16), picker, preferred_element_type=F32)
    at = chunk_at * CH + upto.astype(jnp.int32) - 1
    ends[...] = jnp.clip(jnp.where(there > 0.5, at, SLOTS), 0, SLOTS)


def tile_pass(n, c, tiles, left, order, same, run_ref, first=0, dates=DATES):
    zeros = jnp.zeros((dates, BLOCK), BF16)
    lines = slice(first, first + dates)
    contract = (((1,), (1,)), ((), ())) if n == 0 else (((1,), (0,)), ((), ()))

    def step(g, run):
        for u in range(0, UNROLL, 2):
            s = c * CH + g * UNROLL + u
            pair = jnp.concatenate([tiles[order[0, s]], tiles[order[0, s + 1]]], axis=1 - n)
            lhs = jnp.concatenate(
                [
                    jnp.concatenate([left[order[1, s]], zeros], axis=1),
                    jnp.concatenate([zeros, left[order[1, s + 1]]], axis=1),
                ],
                axis=0,
            )
            prod = lax.dot_general(lhs, pair, contract, preferred_element_type=F32)
            run = prod[0:dates] + run * same[0, s]
            run_ref[s, lines] = run
            run = prod[dates:] + run * same[0, s + 1]
            run_ref[s + 1, lines] = run
        return run

    lax.fori_loop(0, CH // UNROLL, step, jnp.zeros((dates, BLOCK), F32))


def gathered(line, run_ref, ends, first, dates):
    lines = slice(first, first + dates)
    total = run_ref[ends[line, 0], lines]
    for c in range(1, CHUNKS):
        total += run_ref[ends[line, c], lines]
    return total


def curvature_of(edges, window, base):
    e_at = iota((WIN, 2 * BLOCK), 1)
    block_at = (iota((WIN, 2 * BLOCK), 0) + base + 128 - HALO) % 128
    anchor = block_at * BLOCK + e_at // 2
    delta = edges[:, 0, :] + edges[:, 1, :] - 2 * anchor
    delta = (delta + 3 * PATCHES // 2 + PATCHES) % PATCHES - PATCHES // 2
    delta = jnp.concatenate([delta.astype(F32), jnp.zeros((16 - WIN, 2 * BLOCK), F32)], axis=0).astype(BF16)
    rows, cols = [], []
    for j in range(2):
        pick = (iota((2 * BLOCK, BLOCK), 0) == 2 * iota((2 * BLOCK, BLOCK), 1) + j).astype(F32).astype(BF16)
        pick_t = (iota((BLOCK, 2 * BLOCK), 1) == 2 * iota((BLOCK, 2 * BLOCK), 0) + j).astype(F32).astype(BF16)
        rows.append(jnp.dot(delta, pick, preferred_element_type=F32) + iota((16, BLOCK), 1).astype(F32))
        cols.append(
            lax.dot_general(pick_t, delta, (((1,), (1,)), ((), ())), preferred_element_type=F32)
            + iota((BLOCK, 16), 0).astype(F32)
        )
    q_at = iota((BLOCK, BLOCK), 1).astype(F32)
    p_at = iota((BLOCK, BLOCK), 0).astype(F32)
    smooth, middle, degree_mid = [], None, None
    for cq in range(HALO // 2, HALO // 2 + HALO + 1):
        blocks = []
        for cp in range(cq - 2, cq + 3):
            off = float((cq - cp) * BLOCK)
            adj = jnp.zeros((BLOCK, BLOCK), F32)
            for j in range(2):
                adj += jnp.where(cols[j][:, cp : cp + 1] == q_at + off, 1.0, 0.0)
                adj += jnp.where(rows[j][cq : cq + 1, :] == p_at - off, 1.0, 0.0)
            blocks.append(adj.astype(BF16))
        adj = jnp.concatenate(blocks, axis=0)
        around = jnp.dot(window[:, (cq - 2) * BLOCK : (cq + 3) * BLOCK], adj, preferred_element_type=F32)
        degree = around[DATES : DATES + 1]
        own = window[0:DATES, cq * BLOCK : (cq + 1) * BLOCK].astype(F32)
        smooth.append(degree * own - around[0:DATES])
        if cq == HALO:
            middle, degree_mid = adj, degree
    field = jnp.concatenate(smooth, axis=1)
    high = field.astype(BF16)
    low = (field - high.astype(F32)).astype(BF16)
    around = jnp.dot(high, middle, preferred_element_type=F32) + jnp.dot(low, middle, preferred_element_type=F32)
    return 0.05 * (degree_mid * smooth[HALO // 2] - around)


def kernel(
    tiles_h, row_h, col_h, count_h, slip_h, obs_h, edge_h, resid_h, grad_ref,
    tb0, tb1, row_v, col_v, count_v, slip_v, slip_blk, ext, obs_v, edges_v,
    order_v0, same_v0, ends_v0, order_v1, same_v1, ends_v1, order0, same0, ends0, order1, same1, ends1, run_ref,
    sib_send, sib_recv, chip_sum, zl_recv, resid_v, resid_blk0, resid_blk1, curve_v,
    rs_send, rs_recv, z_send, z_recv,
    tile_sem, in_sem, edge_sem, sm_sem, out_sem,
    sib_ss, sib_rs, halo_ss, halo_rs, zl_ss, zl_rs, res_ss, res_rs, rs_ss, rs_rs, z_ss, z_rs,
):
    ps, pt = lax.axis_index("ps"), lax.axis_index("patch")
    y, zh, x = ps // 16, ps // 4 % 4, ps % 4
    core = pt % 2
    par = x % 2
    tbs = (tb0, tb1)
    tables_v = ((order_v0, same_v0, ends_v0), (order_v1, same_v1, ends_v1))
    tables = ((order0, same0, ends0), (order1, same1, ends1))
    order, same, ends = zip(*tables)
    resid_blks = (resid_blk0, resid_blk1)

    def at(yy, zz, xx):
        return (yy * 16 + zz * 4 + xx, pt)

    sibling = (ps, pt + 1 - 2 * core)
    across = (ps, (pt + 2) % 4)
    after = (ps, (pt + 1) % 4)
    before = (ps, (pt + 3) % 4)

    small = [
        pltpu.make_async_copy(row_h, row_v, in_sem.at[0]),
        pltpu.make_async_copy(col_h, col_v, in_sem.at[1]),
        pltpu.make_async_copy(count_h, count_v, in_sem.at[2]),
    ]
    slip_in = pltpu.make_async_copy(slip_h, slip_v, in_sem.at[3])
    for copy in small:
        copy.start()
    slip_in.start()
    tile_in = [
        pltpu.make_async_copy(tiles_h.at[pl.ds(c * CH, CH)], tbs[c], tile_sem.at[c]) for c in range(CHUNKS)
    ]
    for copy in tile_in:
        copy.start()
    obs_in = pltpu.make_async_copy(
        obs_h.at[:, pl.ds(pl.multiple_of(core * HALF, HALF), HALF)], obs_v, in_sem.at[4]
    )
    obs_in.start()
    base = pt * COLS + ps // 2
    edge_in = []
    for w in range(WIN):
        block = (base + 128 - HALO + w) % 128
        edge_in.append(
            pltpu.make_async_copy(
                edge_h.at[:, pl.ds(pl.multiple_of(block * 256, 256), 256)], edges_v.at[w], edge_sem.at[w]
            )
        )
    for copy in edge_in:
        copy.start()

    barrier = pltpu.get_barrier_semaphore()
    partners = [(ps, (pt + k) % 4) for k in (1, 2, 3)]
    partners += [at(xor(y, n), zh, xor(x, m)) for n in range(4) for m in range(4) if n or m]
    partners += [at(y, xor(zh, m), x) for m in (1, 2, 3)]
    for device in partners:
        pl.semaphore_signal(barrier, inc=1, device_id=device, device_id_type=MESH)

    for copy in small:
        copy.wait()

    def sort_by(n):
        sort_slots(n, row_v, col_v, count_v, *tables_v[n])
        staged = [
            pltpu.make_async_copy(here, there, sm_sem.at[3 * n + i])
            for i, (here, there) in enumerate(zip(tables_v[n], tables[n], strict=True))
        ]
        for copy in staged:
            copy.start()
        return staged

    staged = sort_by(0)
    slip_in.wait()
    for k in range(COLS):
        slip_blk[k] = slip_v[:, k * BLOCK : (k + 1) * BLOCK]
    run_ref[SLOTS] = jnp.zeros((DATES, BLOCK), F32)
    for copy in staged:
        copy.wait()

    for c in range(CHUNKS):
        tile_in[c].wait()
        tile_pass(0, c, tbs[c], slip_blk, order[0], same[0], run_ref)

    pl.semaphore_wait(barrier, len(partners))

    def remote(src, dst, ss, rs, device):
        return pltpu.make_async_remote_copy(
            src_ref=src, dst_ref=dst, send_sem=ss, recv_sem=rs, device_id=device, device_id_type=MESH
        )

    sib = []
    for g, (first, dates) in enumerate(GROUPS):
        for k in range(8):
            sib_send[first : first + dates, k * BLOCK : (k + 1) * BLOCK] = gathered(
                (1 - core) * 8 + k, run_ref, ends[0], first, dates
            )
        lines = pl.ds(first, dates)
        sib.append(remote(sib_send.at[lines], sib_recv.at[lines], sib_ss.at[g], sib_rs.at[g], sibling))
        sib[g].start()
    halo = [
        remote(
            slip_v.at[:, pl.ds(K_DEV - HALO * BLOCK, HALO * BLOCK)],
            ext.at[pl.ds(0, DATES), pl.ds(0, HALO * BLOCK)],
            halo_ss.at[0], halo_rs.at[0], after,
        ),
        remote(
            slip_v.at[:, pl.ds(0, HALO * BLOCK)],
            ext.at[pl.ds(0, DATES), pl.ds(HALO * BLOCK + K_DEV, HALO * BLOCK)],
            halo_ss.at[1], halo_rs.at[1], before,
        ),
    ]
    zl = []
    for k in range(8):
        chip_sum[:, k * BLOCK : (k + 1) * BLOCK] = gathered(core * 8 + k, run_ref, ends[0], 0, DATES)
    for g, (first, dates) in enumerate(GROUPS):
        sib[g].wait_recv()
        lines = pl.ds(first, dates)
        chip_sum[lines] = chip_sum[lines] + sib_recv[lines]
        zl.append(remote(chip_sum.at[lines], zl_recv.at[lines], zl_ss.at[g], zl_rs.at[g], across))
        zl[g].start()
    for copy in halo:
        copy.start()
    staged = sort_by(1)
    ext[0:DATES, HALO * BLOCK : HALO * BLOCK + K_DEV] = slip_v[...]
    ext[DATES:, :] = jnp.ones((16, K_DEV + 2 * HALO * BLOCK), BF16)
    obs_in.wait()
    for copy in edge_in:
        copy.wait()
    for copy in staged:
        copy.wait()

    res, outs, plane = [], [], {}

    def own_half(g):
        first, dates = GROUPS[g]
        lines = pl.ds(first, dates)
        zl[g].wait_recv()
        value = chip_sum[lines] + zl_recv[lines] - obs_v[lines]
        resid_v[core, lines] = value
        res.append(
            remote(resid_v.at[core, lines], resid_v.at[core, lines], res_ss.at[g], res_rs.at[g], sibling)
        )
        res[g].start()
        for k in range(8):
            resid_blks[g][core * 8 + k] = value[:, k * BLOCK : (k + 1) * BLOCK].astype(BF16)

    def other_half(g):
        first, dates = GROUPS[g]
        res[g].wait_recv()
        value = resid_v[1 - core, pl.ds(first, dates)]
        for k in range(8):
            resid_blks[g][(1 - core) * 8 + k] = value[:, k * BLOCK : (k + 1) * BLOCK].astype(BF16)

    def to_plane(g, part, pairs):
        first, dates = GROUPS[g]
        lines = slice(first, first + dates)
        low = iota((dates, BLOCK), 1) < 64
        lanes_sent = pl.ds(pairs[0] * BLOCK, len(pairs) * BLOCK)
        for n in (2, 1, 3, 0):
            for mb in (2, 0):
                line = xor(y, n) * 8 + xor(x, mb) // 2
                for pair in pairs:
                    b0 = gathered(line + 4 * pair, run_ref, ends[1], first, dates)
                    b1 = gathered(line + 4 * pair + 2, run_ref, ends[1], first, dates)
                    lanes = slice(pair * BLOCK, (pair + 1) * BLOCK)
                    rs_send[n * 4 + mb + par, lines, lanes] = jnp.where(low, b0, pltpu.roll(b1, 64, 1))
                    rs_send[n * 4 + mb + 1 - par, lines, lanes] = jnp.where(low, pltpu.roll(b0, 64, 1), b1)
                for m in (mb, mb + 1):
                    if n or m:
                        i = n * 4 + m
                        plane[part, i] = remote(
                            rs_send.at[i, pl.ds(first, dates), lanes_sent],
                            rs_recv.at[i, pl.ds(first, dates), lanes_sent],
                            rs_ss.at[part, i], rs_rs.at[part, i], at(xor(y, n), zh, xor(x, m)),
                        )
                        plane[part, i].start()

    def from_plane(g, part, pairs):
        first, dates = GROUPS[g]
        lines = slice(first, first + dates)
        lanes = slice(pairs[0] * BLOCK, (pairs[-1] + 1) * BLOCK)
        total = rs_send[0, lines, lanes]
        for i in (1, 4, 3, 12, 5, 7, 13, 15, 2, 8, 6, 9, 14, 11, 10):
            plane[part, i].wait_recv()
            total = total + rs_recv[i, lines, lanes]
        return total

    own_half(0)
    other_half(0)
    tile_pass(1, 0, tbs[0], resid_blks[0], order[1], same[1], run_ref, *GROUPS[0])
    own_half(1)
    tile_pass(1, 1, tbs[1], resid_blks[0], order[1], same[1], run_ref, *GROUPS[0])
    to_plane(0, 0, (0, 1))
    other_half(1)
    for q in range(2):
        outs.append(pltpu.make_async_copy(resid_v.at[q], resid_h.at[:, pl.ds(q * HALF, HALF)], out_sem.at[q]))
        outs[q].start()
    for c in range(CHUNKS):
        tile_pass(1, c, tbs[c], resid_blks[1], order[1], same[1], run_ref, *GROUPS[1])
    to_plane(1, 1, (0,))
    to_plane(1, 2, (1,))

    for copy in halo:
        copy.wait_recv()
    window = ext[:, pl.ds(pl.multiple_of((ps // 2) * BLOCK, BLOCK), WIN * BLOCK)]
    curve_v[...] = curvature_of(edges_v, window, base)

    total = from_plane(0, 0, (0, 1))
    half = DATES // 2
    low_half = iota((half, BLOCK), 1) < 64

    def pack(block, odd):
        top, bottom = block[0:half], block[half:]
        if odd:
            return jnp.where(low_half, pltpu.roll(top, 64, 1), bottom)
        return jnp.where(low_half, top, pltpu.roll(bottom, 64, 1))

    line = {}
    for m in (1, 2, 3):
        line[m] = remote(z_send.at[xor(zh, m)], z_recv.at[m], z_ss.at[m], z_rs.at[m], at(y, xor(zh, m), x))

    for pair in range(2):
        block = jnp.concatenate(
            [total[:, pair * BLOCK : (pair + 1) * BLOCK], from_plane(1, 1 + pair, (pair,))], axis=0
        )
        for odd in range(2):
            z_send[2 * pair + odd] = pack(block, odd)

        @pl.when(zh // 2 == pair)
        def near_by():
            line[1].start()

        @pl.when(zh // 2 != pair)
        def far():
            line[2].start()
            line[3].start()

    for copy in outs:
        copy.wait()
    for copy in [*sib, *halo, *zl, *res, *plane.values()]:
        copy.wait_send()
    curve = curve_v[...]
    share = z_send[zh] + jnp.where(ps % 2 == 0, pack(curve, 0), pack(curve, 1))
    for m in (1, 3, 2):
        line[m].wait_recv()
        share = share + z_recv[m]
    grad_ref[0:half, :] = share[:, 0:64]
    grad_ref[half:, :] = pltpu.roll(share, 64, 1)[:, 0:64]

    for copy in line.values():
        copy.wait_send()


def body(tiles, tile_row, tile_col, tile_count, slip, observations, edge_list):
    any_spec = pl.BlockSpec(memory_space=pltpu.HBM)
    vmem, dma = pltpu.VMEM, pltpu.SemaphoreType.DMA
    i32 = jnp.int32
    near = functools.partial(pltpu.with_memory_space_constraint, memory_space=pltpu.HBM)
    resid, grad = pl.pallas_call(
        kernel,
        out_shape=(
            jax.ShapeDtypeStruct((DATES, ROWS * BLOCK), F32),
            jax.ShapeDtypeStruct((DATES, 64), F32),
        ),
        in_specs=[any_spec] * 7,
        out_specs=(any_spec, pl.BlockSpec(memory_space=vmem)),
        scratch_shapes=[
            *[vmem((CH, BLOCK, BLOCK), BF16) for _ in range(CHUNKS)],
            vmem((1, 1, SLOTS), i32),
            vmem((1, 1, SLOTS), i32),
            vmem((1, 1), i32),
            vmem((DATES, K_DEV), BF16),
            vmem((COLS, DATES, BLOCK), BF16),
            vmem((DATES + 16, K_DEV + 2 * HALO * BLOCK), BF16),
            vmem((DATES, HALF), F32),
            vmem((WIN, 2, 256), i32),
            *[vmem((8, SLOTS), i32), vmem((8, SLOTS), F32), vmem((COLS, 128), i32)] * 2,
            *[pltpu.SMEM((8, SLOTS), i32), pltpu.SMEM((8, SLOTS), F32), pltpu.SMEM((COLS, 128), i32)] * 2,
            vmem((SLOTS + 1, DATES, BLOCK), F32),
            *[vmem((DATES, HALF), F32) for _ in range(4)],
            vmem((2, DATES, HALF), F32),
            *[vmem((ROWS, dates, BLOCK), BF16) for _, dates in GROUPS],
            vmem((DATES, BLOCK), F32),
            vmem((16, DATES, 256), F32),
            vmem((16, DATES, 256), F32),
            vmem((4, DATES // 2, BLOCK), F32),
            vmem((4, DATES // 2, BLOCK), F32),
            dma((CHUNKS,)), dma((5,)), dma((WIN,)), dma((6,)), dma((2,)),
            dma((2,)), dma((2,)), dma((2,)), dma((2,)), dma((2,)), dma((2,)), dma((2,)), dma((2,)),
            dma((3, 16)), dma((3, 16)), dma((4,)), dma((4,)),
        ],
        compiler_params=pltpu.CompilerParams(
            collective_id=0, has_side_effects=True, vmem_limit_bytes=48 * 2**20
        ),
        cost_estimate=pl.CostEstimate(flops=2 * 10**9, bytes_accessed=10 * 2**20, transcendentals=0),
    )(
        *(near(a) for a in (tiles[0, 0], tile_row, tile_col)),
        tile_count,
        *(near(a) for a in (slip, observations, edge_list)),
    )
    return placed(resid, grad)


def placed(resid, grad):
    def copies(resid_in, grad_in, resid_out, grad_out, sem):
        moves = [
            pltpu.make_async_copy(resid_in, resid_out, sem.at[0]),
            pltpu.make_async_copy(grad_in, grad_out, sem.at[1]),
        ]
        for move in moves:
            move.start()
        for move in moves:
            move.wait()

    return pl.pallas_call(
        copies,
        out_shape=tuple(jax.ShapeDtypeStruct(a.shape, a.dtype) for a in (resid, grad)),
        in_specs=[pl.BlockSpec(memory_space=pl.ANY)] * 2,
        out_specs=(pl.BlockSpec(memory_space=pl.ANY),) * 2,
        scratch_shapes=[pltpu.SemaphoreType.DMA((2,))],
        compiler_params=pltpu.CompilerParams(vmem_limit_bytes=2**20),
    )(resid, grad)


def solution(mesh):
    in_specs = (
        P("ps", "patch", None, None, None),
        P("ps", "patch", None),
        P("ps", "patch", None),
        P("ps", "patch"),
        P(None, "patch"),
        P(None, "ps"),
        P(),
    )
    out_specs = (P(None, "ps"), P(None, ("patch", "ps")))
    return jax.shard_map(body, mesh=mesh, in_specs=in_specs, out_specs=out_specs, check_vma=False)
```
